256 devices in a mesh: leaf: 32 (over x, z), fac: 8 (over y, core).
Axes of the slice: x: 4, y: 4, z: 8, core: 2. Of those that a mesh axis runs over, the one named last changes fastest.
Arguments:
- loads: bfloat16 [256, 131072], P(None, ('leaf', 'fac')), may hold values from -6 to 6
- leaf_sizes: int32 [32], P('leaf'), may hold values from 2048 to 4096, as said below
- tree_order: int32 [32, 4096], P('leaf'), may hold values from 0 to 4095, each once within a row
- leaf_inverse: bfloat16 [131072, 4096], P(('leaf', 'fac')), may hold values from -0.09375 to 0.09375
- left_factors: bfloat16 [3, 131072, 128], P(None, ('leaf', 'fac')), may hold values from -0.5 to 0.5
- right_factors: bfloat16 [3, 131072, 128], P(None, ('leaf', 'fac')), may hold values from -0.0234375 to 0.0234375
Outputs:
- solution: float32 [256, 131072], P(None, ('leaf', 'fac'))
The draws below stay inside these ranges and needn't reach their ends.
Inputs may be any that keep to these rules, and one draw needn't show every extreme that they name: `leaf_sizes`: some leaf cluster is full in every draw. `tree_order`: each row is a permutation of the cluster's slots.
All inputs are finite; a program needn't handle non-finite values.
Results may differ from the reference program's by a relative error of at most 0.0003.
Values may be sent and summed in bfloat16 or wider, within the bound.
A program may use at most 64 MiB of HBM per device.

```python
import jax
import jax.numpy as jnp
from jax import lax

CASES = 256
RANK = 128
LEVELS = 3
LEAF_ROWS = 4096
ROWS_ALL = 131072
N_LEAF = 32


def draw_leaf_sizes(key, part):
    key = jax.random.fold_in(key, 11)
    first, second = jax.random.split(key)
    sizes = jax.random.randint(first, (N_LEAF,), LEAF_ROWS // 2, LEAF_ROWS + 1)
    fullest = jax.random.randint(second, (), 0, N_LEAF)
    return jnp.where(jnp.arange(N_LEAF) == fullest, LEAF_ROWS, sizes).astype(jnp.int32)


def shard_levels(own_key, extent, cuts, least, top_value):
    level, own = 1.0, jax.random.fold_in(own_key, 6)
    for dim, shards_of in cuts:
        heights = jnp.exp(jax.random.uniform(jax.random.fold_in(own, dim), (shards_of,), jnp.float32, least / len(cuts), top_value / len(cuts)))
        level = level * jnp.repeat(heights, extent[dim] // shards_of).reshape([-1 if axis == dim else 1 for axis in range(len(extent))])
    return level


def normal_values(own_key, dims, deviation, reach, cuts=(), held_as=jnp.bfloat16):
    array = jax.random.normal(own_key, dims, jnp.float32) * deviation
    if len(cuts) > 0:
        array = shard_levels(own_key, dims, cuts, -0.22, 0.18) * array
    return jnp.clip(array, min=-reach, max=reach).astype(held_as)


def setup_inputs(seed: int = 0) -> dict:
    seeds = jax.random.split(jax.random.key(seed), 7)
    loads = normal_values(seeds[0], (CASES, ROWS_ALL), 1.0, 6.0, ((1, 256),))
    leaf_sizes = draw_leaf_sizes(jax.random.fold_in(seeds[6], 71), 0)
    tree_order = jax.vmap(lambda own: jax.random.permutation(own, LEAF_ROWS))(jax.random.split(seeds[2], N_LEAF)).reshape((N_LEAF, LEAF_ROWS)).astype(jnp.int32)
    leaf_inverse = normal_values(seeds[3], (ROWS_ALL, LEAF_ROWS), LEAF_ROWS ** -0.5, 0.09375, ((0, 256),))
    left_factors = normal_values(seeds[4], (LEVELS, ROWS_ALL, RANK), RANK ** -0.5, 0.5, ((1, 256),))
    right_factors = normal_values(seeds[5], (LEVELS, ROWS_ALL, RANK), (ROWS_ALL // 2) ** -0.5, 0.0234375, ((1, 256),))
    return {"loads": loads, "leaf_sizes": leaf_sizes, "tree_order": tree_order, "leaf_inverse": leaf_inverse, "left_factors": left_factors, "right_factors": right_factors}


def reference(loads, leaf_sizes, tree_order, leaf_inverse, left_factors, right_factors):
    leaf_count = N_LEAF
    bits = leaf_count.bit_length() - 1
    position = jnp.arange(LEAF_ROWS, dtype=jnp.int32)
    live = (position[None, :] < leaf_sizes[:, None]).astype(jnp.float32)
    grouped = loads.reshape(CASES, leaf_count, LEAF_ROWS)
    ordered = jnp.take_along_axis(grouped, tree_order[None, :, :], axis=2)
    ordered = jnp.where(live[None] > 0, ordered, jnp.zeros_like(ordered))
    blocks = leaf_inverse.reshape(leaf_count, LEAF_ROWS, LEAF_ROWS)

    def leaf_apply(pair):
        rhs, block = pair
        return lax.dot_general(rhs, block, (((1,), (1,)), ((), ())), preferred_element_type=jnp.float32)

    field = lax.map(leaf_apply, (jnp.transpose(ordered, (1, 0, 2)), blocks))
    field = field * live[:, None, :]
    leaf_ids = jnp.arange(leaf_count, dtype=jnp.int32)
    for level in range(LEVELS):
        bit = bits - LEVELS + level
        right = right_factors[level].reshape(leaf_count, LEAF_ROWS, RANK).astype(jnp.float32)
        left = left_factors[level].reshape(leaf_count, LEAF_ROWS, RANK).astype(jnp.float32)
        coef = jnp.einsum("qcl,qlk->qck", field, right, precision=lax.Precision.HIGHEST)
        node = coef.reshape(leaf_count >> bit, 1 << bit, CASES, RANK).sum(axis=1)
        partner = node[jnp.bitwise_xor(jnp.right_shift(leaf_ids, bit), 1)]
        field = (field + jnp.einsum("qck,qlk->qcl", partner, left, precision=lax.Precision.HIGHEST)) * live[:, None, :]
    return jnp.transpose(field, (1, 0, 2)).reshape(CASES, ROWS_ALL)
```

```python
import functools

import jax
import jax.numpy as jnp
from jax import lax
from jax.experimental import pallas as pl
from jax.experimental.pallas import tpu as pltpu
from jax.sharding import PartitionSpec as P

CASES = 256
RANK = 128
LEVELS = 3
SLOTS = 4096
ROWS = 512
HALF = 256
WIDE = LEVELS * RANK
COPIES = 64
MESH = pl.DeviceIdType.MESH


def kernel(
    loads_ref, size_ref, order_ref, inverse_ref, left_ref, right_ref, out_ref,
    raw, blocks, order, match, ordered, inverse, left, right, left_t, right_w,
    field, coef, coef_core, coef_y, coef_mine, in_core, in_y, in_z, sent, in_node, partner,
    mix, mix_core, mix_half, mix_near, mix_far, mix_z, mix_y, mixing,
    local_sem, send_sem, recv_sem,
):
    leaf, fac = lax.axis_index("leaf"), lax.axis_index("fac")
    x, z = lax.div(leaf, 8), lax.rem(leaf, 8)
    y, core = lax.div(fac, 2), lax.rem(fac, 2)
    z_hi, z_lo = lax.div(z, 4), lax.rem(z, 4)
    x_pair = x + 1 - 2 * lax.rem(x, 2)
    x_far = [lax.rem(x + 2, 4), 3 - x]

    def at(x_=x, z_=z, y_=y, core_=core):
        return (x_ * 8 + z_, y_ * 2 + core_)

    def y_off(o):
        return lax.rem(y + o, 4)

    def z_off(o, flip=0):
        return lax.rem(z_hi + flip, 2) * 4 + lax.rem(z_lo + o, 4)

    sibling = at(core_=1 - core)
    near_z = [z_off(o) for o in (1, 2, 3)]
    flip_z = [z_off(o, 1) for o in range(4)]
    z_all = [z_off(o, f) for f in range(2) for o in range(4)]
    partners = [sibling]
    partners += [at(y_=y_off(o)) for o in (1, 2, 3)]
    partners += [at(z_=other) for other in near_z + flip_z]
    partners += [at(z_=other, core_=1 - core) for other in near_z]
    partners += [at(x_=x_pair, z_=other) for other in z_all]
    partners += [at(x_=far, z_=z_off(0, f)) for far in x_far for f in range(2)]

    barrier = pltpu.get_barrier_semaphore()
    for other in partners:
        pl.semaphore_signal(barrier, inc=1, device_id=other, device_id_type=MESH)

    copies = []

    def send(src, dst, target):
        i = len(copies)
        copy = pltpu.make_async_remote_copy(
            src_ref=src, dst_ref=dst, send_sem=send_sem.at[i], recv_sem=recv_sem.at[i],
            device_id=target, device_id_type=MESH,
        )
        copies.append(copy)
        copy.start()
        return copy

    def fetch(i, src, dst):
        copy = pltpu.make_async_copy(src, dst, local_sem.at[i])
        copy.start()
        return copy

    got_loads = fetch(0, loads_ref, raw)
    got_order = fetch(1, order_ref, order)
    got_left = fetch(2, left_ref, left)
    got_right = fetch(3, right_ref, right)
    got_inverse = fetch(4, inverse_ref, inverse)

    got_loads.wait()
    blocks[fac] = raw[...].T
    pl.semaphore_wait(barrier, len(partners))

    def half(block, h):
        return blocks.at[block, pl.ds(h * HALF, HALF), :]

    def pass_on(block, h, target):
        return send(half(block, h), half(block, h), target)

    def block_of(y_, core_=core):
        return y_ * 2 + core_

    up, down = y_off(1), y_off(3)
    up_first = pass_on(fac, 0, at(y_=up))
    down_first = pass_on(fac, 1, at(y_=down))
    own_sib = send(blocks.at[fac], blocks.at[fac], sibling)
    up_second = pass_on(fac, 1, at(y_=up))
    down_second = pass_on(fac, 0, at(y_=down))

    size = size_ref[0]
    got_order.wait()

    @pl.loop(0, 32)
    def _(r):
        place = r * 128 + lax.broadcasted_iota(jnp.int32, (1, 128), 1)
        row = jnp.where(place < size, order[pl.ds(r, 1), :], -1)
        match[pl.ds(pl.multiple_of(r * 128, 128), 128), :] = jnp.broadcast_to(row, (128, 128)).T

    first_row = fac * ROWS

    def permute(parts, first=False):
        @pl.loop(0, 2)
        def _(m):
            rows = pl.ds(pl.multiple_of(m * 2048, 2048), 2048)
            slot = match[rows, :]
            total = None
            for block, start, count in parts:
                picks = []
                for j in range(count // 128):
                    here = block * ROWS + start + j * 128
                    column = here + lax.broadcasted_iota(jnp.int32, (2048, 128), 1)
                    picks.append(jnp.where(slot == column, 1.0, 0.0).astype(jnp.bfloat16))
                term = jnp.dot(
                    jnp.concatenate(picks, axis=1), blocks[block, pl.ds(start, count), :],
                    preferred_element_type=jnp.float32,
                )
                total = term if total is None else total + term
            total = total.astype(jnp.bfloat16)
            if first:
                ordered[rows, :] = total
            else:
                ordered[rows, :] += total

    got_left.wait()
    got_right.wait()
    for level in range(LEVELS):
        live = first_row + lax.broadcasted_iota(jnp.int32, (RANK, ROWS), 1) < size
        turned = left[level].T
        left_t[level * RANK:(level + 1) * RANK, :] = jnp.where(live, turned, jnp.zeros_like(turned))
        right_w[:, level * RANK:(level + 1) * RANK] = right[level]
    mix[:, :2 * RANK] = jnp.dot(left_t[:RANK, :], right_w[:, RANK:], preferred_element_type=jnp.float32)
    mix[:, 2 * RANK:] = jnp.dot(left_t[RANK:2 * RANK, :], right_w[:, 2 * RANK:], preferred_element_type=jnp.float32)
    mix_sib = send(mix.at[pl.ds(pl.multiple_of(64 * (1 - core), 64), 64), :], mix_core, sibling)

    permute([(fac, 0, ROWS)], first=True)

    mix_sib.wait_recv()
    mix_half[...] = mix[pl.ds(pl.multiple_of(64 * core, 64), 64), :] + mix_core[...]
    to_z = []
    for o in range(4):
        rows = pl.ds(pl.multiple_of(16 * lax.rem(z_lo + o, 4), 16), 16)
        to_z.append(send(mix_half.at[rows, pl.ds(0, 2 * RANK)], mix_near.at[o], at(z_=z_off(o, 1))))
        for f in range(2):
            to_z.append(send(
                mix_half.at[rows, pl.ds(2 * RANK, RANK)], mix_far.at[f * 4 + o],
                at(x_=x_pair, z_=z_off(o, f)),
            ))

    own_sib.wait_recv()
    other = block_of(y, 1 - core)
    permute([(other, 0, ROWS)])

    def stage(from_down, h_down, from_up, h_up, block_down, block_up):
        from_down.wait_recv()
        relay_down = pass_on(block_down, h_down, sibling)
        from_up.wait_recv()
        relay_up = pass_on(block_up, h_up, sibling)
        return relay_down, relay_up

    below, above, across = y_off(3), y_off(1), y_off(2)
    up_first.wait_recv()
    relay_a = pass_on(block_of(below), 0, sibling)
    forward_up = pass_on(block_of(below), 0, at(y_=up))
    down_first.wait_recv()
    relay_b = pass_on(block_of(above), 1, sibling)
    forward_down = pass_on(block_of(above), 1, at(y_=down))
    permute([(block_of(below), 0, HALF), (block_of(above), HALF, HALF)])
    relay_a.wait_recv()
    relay_b.wait_recv()
    permute([(block_of(below, 1 - core), 0, HALF), (block_of(above, 1 - core), HALF, HALF)])

    for copy in to_z:
        copy.wait_recv()
    mix_z[:, :2 * RANK] = mix_near[0] + mix_near[1] + mix_near[2] + mix_near[3]
    far = mix_far[0]
    for j in range(1, 8):
        far = far + mix_far[j]
    mix_z[:, 2 * RANK:] = far

    relay_a, relay_b = stage(up_second, 1, down_second, 0, block_of(below), block_of(above))
    permute([(block_of(below), HALF, HALF), (block_of(above), 0, HALF)])
    relay_a.wait_recv()
    relay_b.wait_recv()
    permute([(block_of(below, 1 - core), HALF, HALF), (block_of(above, 1 - core), 0, HALF)])

    relay_a, relay_b = stage(forward_up, 0, forward_down, 1, block_of(across), block_of(across))
    mix_across = [send(mix_z, mix_y.at[o], at(y_=y_off(o))) for o in (1, 2, 3)]
    permute([(block_of(across), 0, ROWS)])
    relay_a.wait_recv()
    relay_b.wait_recv()
    permute([(block_of(across, 1 - core), 0, ROWS)])

    got_inverse.wait()
    solved = jnp.dot(inverse[...], ordered[...], preferred_element_type=jnp.float32)
    live = first_row + lax.broadcasted_iota(jnp.int32, (ROWS, CASES), 0) < size
    field[...] = jnp.where(live, solved, 0.0).T

    def split_dot(value, weight):
        high = value.astype(jnp.bfloat16)
        low = (value - high.astype(jnp.float32)).astype(jnp.bfloat16)
        return jnp.dot(high, weight, preferred_element_type=jnp.float32) + jnp.dot(
            low, weight, preferred_element_type=jnp.float32
        )

    coef[...] = split_dot(field[...], right_w[...])
    to_core = send(coef.at[pl.ds(pl.multiple_of(128 * (1 - core), 128), 128), :], in_core, sibling)

    for copy in mix_across:
        copy.wait_recv()
    mine = pl.ds(pl.multiple_of(64 * core + 16 * z_lo, 16), 16)
    mixing[mine, :] = mix_z[...] + mix_y[1] + mix_y[2] + mix_y[3]
    spread = [send(mixing.at[mine, :], mixing.at[mine, :], at(z_=other)) for other in near_z]
    spread += [
        send(mixing.at[mine, :], mixing.at[mine, :], at(z_=other, core_=1 - core))
        for other in [z] + near_z
    ]

    to_core.wait_recv()
    coef_core[...] = coef[pl.ds(pl.multiple_of(128 * core, 128), 128), :] + in_core[...]
    to_y = [
        send(coef_core.at[pl.ds(pl.multiple_of(32 * y_off(o), 32), 32), :], in_y.at[o], at(y_=y_off(o)))
        for o in (1, 2, 3)
    ]
    for copy in to_y:
        copy.wait_recv()
    coef_y[...] = coef_core[pl.ds(pl.multiple_of(32 * y, 32), 32), :] + in_y[1] + in_y[2] + in_y[3]
    to_z = [
        send(
            coef_y.at[pl.ds(pl.multiple_of(8 * lax.rem(z_lo + o, 4), 8), 8), :], in_z.at[o],
            at(z_=z_off(o)),
        )
        for o in (1, 2, 3)
    ]
    for copy in spread:
        copy.wait_recv()
    for copy in to_z:
        copy.wait_recv()
    coef_mine[...] = coef_y[pl.ds(pl.multiple_of(8 * z_lo, 8), 8), :] + in_z[1] + in_z[2] + in_z[3]

    def exact_dot(value, weight):
        return jnp.dot(value, weight, precision=lax.Precision.HIGHEST, preferred_element_type=jnp.float32)

    zero = coef_mine[:, :RANK]
    sent[0] = zero
    to_node = [send(sent.at[0], in_node.at[0], at(z_=z_off(0, 1)))]
    mixed = exact_dot(zero, mixing[:, :2 * RANK])
    one = coef_mine[:, RANK:2 * RANK] + mixed[:, :RANK]
    sent[1] = one
    to_node += [send(sent.at[1], in_node.at[1 + f], at(x_=x_pair, z_=z_off(0, f))) for f in range(2)]
    sent[2] = coef_mine[:, 2 * RANK:] + mixed[:, RANK:] + exact_dot(one, mixing[:, 2 * RANK:])
    to_node += [
        send(sent.at[2], in_node.at[3 + 2 * g + f], at(x_=far, z_=z_off(0, f)))
        for g, far in enumerate(x_far) for f in range(2)
    ]
    for copy in to_node:
        copy.wait_recv()
    eight = pl.ds(pl.multiple_of(128 * core + 32 * y + 8 * z_lo, 8), 8)
    partner[eight, :RANK] = in_node[0]
    partner[eight, RANK:2 * RANK] = in_node[1] + in_node[2]
    partner[eight, 2 * RANK:] = (in_node[3] + in_node[4]) + (in_node[5] + in_node[6])
    back = [send(partner.at[eight, :], partner.at[eight, :], at(z_=other)) for other in near_z]
    for copy in back:
        copy.wait_recv()
    many = pl.ds(pl.multiple_of(128 * core + 32 * y, 32), 32)
    back = [send(partner.at[many, :], partner.at[many, :], at(y_=y_off(o))) for o in (1, 2, 3)]
    for copy in back:
        copy.wait_recv()
    most = pl.ds(pl.multiple_of(128 * core, 128), 128)
    back = send(partner.at[most, :], partner.at[most, :], sibling)
    back.wait_recv()
    out_ref[...] = field[...] + split_dot(partner[...], left_t[...])
    for copy in copies:
        copy.wait_send()


def body(loads, leaf_sizes, tree_order, leaf_inverse, left_factors, right_factors):
    f32, bf16 = jnp.float32, jnp.bfloat16
    scratch = [
        ((CASES, ROWS), bf16),
        ((8, ROWS, CASES), bf16),
        ((32, 128), jnp.int32),
        ((SLOTS, 128), jnp.int32),
        ((SLOTS, CASES), bf16),
        ((ROWS, SLOTS), bf16),
        ((LEVELS, ROWS, RANK), bf16),
        ((LEVELS, ROWS, RANK), bf16),
        ((WIDE, ROWS), bf16),
        ((ROWS, WIDE), bf16),
        ((CASES, ROWS), f32),
        ((CASES, WIDE), f32),
        ((128, WIDE), f32),
        ((32, WIDE), f32),
        ((8, WIDE), f32),
        ((128, WIDE), f32),
        ((4, 32, WIDE), f32),
        ((4, 8, WIDE), f32),
        ((3, 8, RANK), f32),
        ((7, 8, RANK), f32),
        ((CASES, WIDE), f32),
        ((RANK, WIDE), f32),
        ((64, WIDE), f32),
        ((64, WIDE), f32),
        ((4, 16, 2 * RANK), f32),
        ((8, 16, RANK), f32),
        ((16, WIDE), f32),
        ((4, 16, WIDE), f32),
        ((RANK, WIDE), f32),
    ]
    anywhere = pl.BlockSpec(memory_space=pl.ANY)
    return pl.pallas_call(
        kernel,
        out_shape=jax.ShapeDtypeStruct((CASES, ROWS), f32),
        in_specs=[
            anywhere, pl.BlockSpec(memory_space=pltpu.SMEM), anywhere, anywhere, anywhere, anywhere,
        ],
        out_specs=pl.BlockSpec(memory_space=pltpu.VMEM),
        scratch_shapes=[pltpu.VMEM(shape, dtype) for shape, dtype in scratch] + [
            pltpu.SemaphoreType.DMA((5,)),
            pltpu.SemaphoreType.DMA((COPIES,)),
            pltpu.SemaphoreType.DMA((COPIES,)),
        ],
        compiler_params=pltpu.CompilerParams(
            collective_id=0, has_side_effects=True, vmem_limit_bytes=48 << 20
        ),
    )(loads, leaf_sizes, tree_order.reshape(32, 128), leaf_inverse, left_factors, right_factors)


def solution(mesh):
    placed = (
        P(None, ("leaf", "fac")),
        P("leaf"),
        P("leaf", None),
        P(("leaf", "fac"), None),
        P(None, ("leaf", "fac"), None),
        P(None, ("leaf", "fac"), None),
    )
    return jax.shard_map(
        body, mesh=mesh, in_specs=placed, out_specs=P(None, ("leaf", "fac")), check_vma=False
    )
```

```python
import functools

import jax
import jax.numpy as jnp
from jax import lax
from jax.experimental import pallas as pl
from jax.experimental.pallas import tpu as pltpu
from jax.sharding import PartitionSpec as P

CASES = 256
RANK = 128
LEVELS = 3
SLOTS = 4096
ROWS = 512
HALF = 256
WIDE = LEVELS * RANK
COPIES = 64
MESH = pl.DeviceIdType.MESH


def kernel(
    loads_ref, size_ref, order_ref, inverse_ref, left_ref, right_ref, out_ref,
    blocks, order, match, ordered, inverse, other_inverse, left, right, left_t, right_w,
    partial, from_core, field, coef, in_core, coef_core, in_y, coef_y, in_z, coef_mine,
    sent, in_node, partner,
    mix, mix_core, mix_half, mix_near, mix_far, mix_z, mix_y, mixing, mix_split,
    local_sem, send_sem, recv_sem,
):
    leaf, fac = lax.axis_index("leaf"), lax.axis_index("fac")
    x, z = lax.div(leaf, 8), lax.rem(leaf, 8)
    y, core = lax.div(fac, 2), lax.rem(fac, 2)
    z_hi, z_lo = lax.div(z, 4), lax.rem(z, 4)
    x_pair = x + 1 - 2 * lax.rem(x, 2)
    x_far = [lax.rem(x + 2, 4), 3 - x]

    def at(x_=x, z_=z, y_=y, core_=core):
        return (x_ * 8 + z_, y_ * 2 + core_)

    def y_off(o):
        return lax.rem(y + o, 4)

    def z_off(o, flip=0):
        return lax.rem(z_hi + flip, 2) * 4 + lax.rem(z_lo + o, 4)

    def rows_of(start, count):
        return pl.ds(pl.multiple_of(start, 8), count)

    sibling = at(core_=1 - core)
    near_z = [z_off(o) for o in (1, 2, 3)]
    flip_z = [z_off(o, 1) for o in range(4)]
    z_all = [z_off(o, f) for f in range(2) for o in range(4)]
    partners = [at(y_=y_off(o)) for o in (1, 3, 2)]
    partners += [sibling]
    partners += [at(z_=other) for other in near_z + flip_z]
    partners += [at(x_=x_pair, z_=other) for other in z_all]
    partners += [at(x_=far, z_=z_off(0, f)) for far in x_far for f in range(2)]

    barrier = pltpu.get_barrier_semaphore()
    for other in partners:
        pl.semaphore_signal(barrier, inc=1, device_id=other, device_id_type=MESH)

    copies = []

    def send(src, dst, target):
        i = len(copies)
        copy = pltpu.make_async_remote_copy(
            src_ref=src, dst_ref=dst, send_sem=send_sem.at[i], recv_sem=recv_sem.at[i],
            device_id=target, device_id_type=MESH,
        )
        copies.append(copy)
        copy.start()
        return copy

    def recv(copy):
        copy.wait_recv()

    def fetch(i, src, dst):
        copy = pltpu.make_async_copy(src, dst, local_sem.at[i])
        copy.start()
        return copy

    got_order = fetch(1, order_ref, order)
    got_loads = fetch(0, loads_ref, blocks.at[3])
    got_left = fetch(2, left_ref, left)
    got_right = fetch(3, right_ref, right)

    pl.semaphore_wait(barrier, len(partners))

    def columns(ref, start, count):
        return ref.at[:, pl.ds(start, count)]

    up, down = at(y_=y_off(1)), at(y_=y_off(3))
    up_first = send(columns(loads_ref, 0, HALF), columns(blocks.at[0], 0, HALF), up)
    down_first = send(columns(loads_ref, HALF, HALF), columns(blocks.at[1], HALF, HALF), down)
    up_second = send(columns(loads_ref, HALF, HALF), columns(blocks.at[0], HALF, HALF), up)
    down_second = send(columns(loads_ref, 0, HALF), columns(blocks.at[1], 0, HALF), down)
    size = size_ref[0]
    first_row = fac * ROWS
    got_left.wait()
    got_right.wait()
    for level in range(LEVELS):
        live = first_row + lax.broadcasted_iota(jnp.int32, (RANK, ROWS), 1) < size
        turned = left[level].T
        left_t[level * RANK:(level + 1) * RANK, :] = jnp.where(live, turned, jnp.zeros_like(turned))
        right_w[:, level * RANK:(level + 1) * RANK] = right[level]
    mix[:, :2 * RANK] = jnp.dot(left_t[:RANK, :], right_w[:, RANK:], preferred_element_type=jnp.float32)
    mix[:, 2 * RANK:] = jnp.dot(left_t[RANK:2 * RANK, :], right_w[:, 2 * RANK:], preferred_element_type=jnp.float32)
    mix_sib = send(mix.at[rows_of(64 * (1 - core), 64), :], mix_core, sibling)

    inverse_sib = []
    for j in range(2):
        rows = pl.ds(j * HALF, HALF)
        inverse_sib.append(send(inverse_ref.at[rows, :], other_inverse.at[rows, :], sibling))
    got_inverse = fetch(4, inverse_ref, inverse)

    got_order.wait()

    @pl.loop(0, 32)
    def _(r):
        place = r * 128 + lax.broadcasted_iota(jnp.int32, (1, 128), 1)
        row = jnp.where(place < size, order[pl.ds(r, 1), :], -1)
        match[pl.ds(pl.multiple_of(r * 128, 128), 128), :] = jnp.broadcast_to(row, (128, 128)).T

    owners = [y_off(3) * 2 + core, y_off(1) * 2 + core, y_off(2) * 2 + core, fac]

    def permute(parts, first=False):
        @pl.loop(0, 2)
        def _(m):
            rows = pl.ds(pl.multiple_of(m * 2048, 2048), 2048)
            slot = match[rows, :]
            total = None
            for block, start, count in parts:
                picks = []
                for j in range(count // 128):
                    here = owners[block] * ROWS + start + j * 128
                    column = here + lax.broadcasted_iota(jnp.int32, (2048, 128), 1)
                    picks.append(jnp.where(slot == column, 1.0, 0.0).astype(jnp.bfloat16))
                picks = picks[0] if len(picks) == 1 else jnp.concatenate(picks, axis=1)
                term = lax.dot_general(
                    picks, blocks[block, :, start:start + count], (((1,), (1,)), ((), ())),
                    preferred_element_type=jnp.float32,
                )
                total = term if total is None else total + term
            total = total.astype(jnp.bfloat16)
            if first:
                ordered[rows, :] = total
            else:
                ordered[rows, :] += total

    recv(mix_sib)
    mix_half[...] = mix[rows_of(64 * core, 64), :] + mix_core[...]
    to_z = []
    for o in range(4):
        rows = rows_of(16 * lax.rem(z_lo + o, 4), 16)
        to_z.append(send(mix_half.at[rows, pl.ds(0, 2 * RANK)], mix_near.at[o], at(z_=z_off(o, 1))))
        for f in range(2):
            to_z.append(send(
                mix_half.at[rows, pl.ds(2 * RANK, RANK)], mix_far.at[f * 4 + o],
                at(x_=x_pair, z_=z_off(o, f)),
            ))

    got_loads.wait()
    permute([(3, 0, ROWS)], first=True)

    forwards = []
    quarter = HALF // 2
    recv(up_first)
    for j in range(2):
        here = j * quarter
        forwards.append(send(columns(blocks.at[0], here, quarter), columns(blocks.at[2], here, quarter), up))
    recv(down_first)
    for j in range(2):
        here = HALF + (1 - j) * quarter
        forwards.append(send(columns(blocks.at[1], here, quarter), columns(blocks.at[2], here, quarter), down))
    permute([(0, 0, HALF), (1, HALF, HALF)])

    recv(up_second)
    recv(down_second)
    permute([(0, HALF, HALF), (1, 0, HALF)])

    for copy in to_z:
        recv(copy)
    mix_z[:, :2 * RANK] = mix_near[0] + mix_near[1] + mix_near[2] + mix_near[3]
    far = mix_far[0]
    for j in range(1, 8):
        far = far + mix_far[j]
    mix_z[:, 2 * RANK:] = far
    mix_across = [send(mix_z, mix_y.at[o], at(y_=y_off(o))) for o in (1, 2, 3)]

    recv(forwards[0])
    recv(forwards[2])
    permute([(2, 0, quarter), (2, 3 * quarter, quarter)])
    recv(forwards[1])
    recv(forwards[3])
    permute([(2, quarter, HALF)])

    to_core = []
    for j in range(2):
        rows = pl.ds(j * HALF, HALF)
        recv(inverse_sib[j])
        partial[rows, :] = jnp.dot(other_inverse[rows, :], ordered[...], preferred_element_type=jnp.float32)
        to_core.append(send(partial.at[rows, :], from_core.at[rows, :], sibling))

    got_inverse.wait()
    solved = jnp.dot(inverse[...], ordered[...], preferred_element_type=jnp.float32)
    for copy in to_core:
        recv(copy)
    live = first_row + lax.broadcasted_iota(jnp.int32, (ROWS, CASES), 0) < size
    field[...] = jnp.where(live, solved + from_core[...], 0.0).T

    def halves(value):
        high = value.astype(jnp.bfloat16)
        return high, (value - high.astype(jnp.float32)).astype(jnp.bfloat16)

    def split_dot(value, weight):
        high, low = halves(value)
        return jnp.dot(high, weight, preferred_element_type=jnp.float32) + jnp.dot(
            low, weight, preferred_element_type=jnp.float32
        )

    theirs, ours = rows_of(128 * (1 - core), 128), rows_of(128 * core, 128)
    coef[...] = split_dot(field[theirs, :], right_w[...])
    coef_sib = send(coef, in_core, sibling)
    own_coef = split_dot(field[ours, :], right_w[...])
    for copy in mix_across:
        recv(copy)
    mine = rows_of(64 * core + 16 * z_lo, 16)
    mixing[mine, :] = mix_z[...] + mix_y[1] + mix_y[2] + mix_y[3]
    spread = [send(mixing.at[mine, :], mixing.at[mine, :], at(z_=other)) for other in near_z]
    recv(coef_sib)
    coef_core[...] = own_coef + in_core[...]
    to_y = [
        send(coef_core.at[rows_of(32 * y_off(o), 32), :], in_y.at[o], at(y_=y_off(o)))
        for o in (2, 1, 3)
    ]
    for copy in spread:
        recv(copy)
    sixty_four = mixing.at[rows_of(64 * core, 64), :]
    spread = send(sixty_four, sixty_four, sibling)
    for copy in to_y:
        recv(copy)
    coef_y[...] = coef_core[rows_of(32 * y, 32), :] + in_y[1] + in_y[2] + in_y[3]
    to_z = [
        send(coef_y.at[rows_of(8 * lax.rem(z_lo + o, 4), 8), :], in_z.at[o], at(z_=z_off(o)))
        for o in (1, 2, 3)
    ]
    recv(spread)
    mix_split[:, :WIDE], mix_split[:, WIDE:] = halves(mixing[...])
    for copy in to_z:
        recv(copy)
    coef_mine[...] = coef_y[rows_of(8 * z_lo, 8), :] + in_z[1] + in_z[2] + in_z[3]

    def mixed(value, start, count):
        high, low = halves(value)
        both = jnp.concatenate([high, low], axis=0)
        by_high = jnp.dot(both, mix_split[:, start:start + count], preferred_element_type=jnp.float32)
        by_low = jnp.dot(both, mix_split[:, WIDE + start:WIDE + start + count], preferred_element_type=jnp.float32)
        return by_high[:8] + (by_high[8:] + by_low[:8])

    zero = coef_mine[:, :RANK]
    sent[0] = zero
    to_node = [send(sent.at[0], in_node.at[0], at(z_=z_off(0, 1)))]
    terms = mixed(zero, 0, 2 * RANK)
    one = coef_mine[:, RANK:2 * RANK] + terms[:, :RANK]
    sent[1] = one
    to_node += [send(sent.at[1], in_node.at[1 + f], at(x_=x_pair, z_=z_off(0, f))) for f in range(2)]
    sent[2] = coef_mine[:, 2 * RANK:] + terms[:, RANK:] + mixed(one, 2 * RANK, RANK)
    to_node += [
        send(sent.at[2], in_node.at[3 + 2 * g + f], at(x_=far, z_=z_off(0, f)))
        for g, far in enumerate(x_far) for f in range(2)
    ]
    for copy in to_node:
        recv(copy)
    eight = rows_of(128 * core + 32 * y + 8 * z_lo, 8)
    partner[eight, :RANK] = in_node[0]
    partner[eight, RANK:2 * RANK] = in_node[1] + in_node[2]
    partner[eight, 2 * RANK:] = (in_node[3] + in_node[4]) + (in_node[5] + in_node[6])
    back = [send(partner.at[eight, :], partner.at[eight, :], at(z_=other)) for other in near_z]
    for copy in back:
        recv(copy)

    def thirty_two(y_):
        return partner.at[rows_of(128 * core + 32 * y_, 32), :]

    back = [(send(thirty_two(y), thirty_two(y), at(y_=y_off(o))), y_off(4 - o)) for o in (2, 1, 3)]
    relays = [send(thirty_two(y), thirty_two(y), sibling)]
    for copy, y_ in back[1:] + back[:1]:
        recv(copy)
        relays.append(send(thirty_two(y_), thirty_two(y_), sibling))
    out_ref[ours, :] = field[ours, :] + split_dot(partner[ours, :], left_t[...])
    for copy in relays:
        recv(copy)
    out_ref[theirs, :] = field[theirs, :] + split_dot(partner[theirs, :], left_t[...])
    for copy in copies:
        copy.wait_send()


def body(loads, leaf_sizes, tree_order, leaf_inverse, left_factors, right_factors):
    f32, bf16 = jnp.float32, jnp.bfloat16
    scratch = [
        ((4, CASES, ROWS), bf16),
        ((32, 128), jnp.int32),
        ((SLOTS, 128), jnp.int32),
        ((SLOTS, CASES), bf16),
        ((ROWS, SLOTS), bf16),
        ((ROWS, SLOTS), bf16),
        ((LEVELS, ROWS, RANK), bf16),
        ((LEVELS, ROWS, RANK), bf16),
        ((WIDE, ROWS), bf16),
        ((ROWS, WIDE), bf16),
        ((ROWS, CASES), f32),
        ((ROWS, CASES), f32),
        ((CASES, ROWS), f32),
        ((128, WIDE), f32),
        ((128, WIDE), f32),
        ((128, WIDE), f32),
        ((4, 32, WIDE), f32),
        ((32, WIDE), f32),
        ((4, 8, WIDE), f32),
        ((8, WIDE), f32),
        ((3, 8, RANK), f32),
        ((7, 8, RANK), f32),
        ((CASES, WIDE), f32),
        ((RANK, WIDE), f32),
        ((64, WIDE), f32),
        ((64, WIDE), f32),
        ((4, 16, 2 * RANK), f32),
        ((8, 16, RANK), f32),
        ((16, WIDE), f32),
        ((4, 16, WIDE), f32),
        ((RANK, WIDE), f32),
        ((RANK, 2 * WIDE), bf16),
    ]
    in_hbm = pl.BlockSpec(memory_space=pltpu.HBM)
    return pl.pallas_call(
        kernel,
        out_shape=pltpu.VMEM((CASES, ROWS), f32),
        in_specs=[
            in_hbm, pl.BlockSpec(memory_space=pltpu.SMEM), in_hbm, in_hbm, in_hbm, in_hbm,
        ],
        out_specs=pl.BlockSpec(memory_space=pltpu.VMEM),
        scratch_shapes=[pltpu.VMEM(shape, dtype) for shape, dtype in scratch] + [
            pltpu.SemaphoreType.DMA((5,)),
            pltpu.SemaphoreType.DMA((COPIES,)),
            pltpu.SemaphoreType.DMA((COPIES,)),
        ],
        compiler_params=pltpu.CompilerParams(
            collective_id=0, has_side_effects=True, vmem_limit_bytes=60 << 20
        ),
    )(loads, leaf_sizes, tree_order.reshape(32, 128), leaf_inverse, left_factors, right_factors)


def solution(mesh):
    placed = (
        P(None, ("leaf", "fac")),
        P("leaf"),
        P("leaf", None),
        P(("leaf", "fac"), None),
        P(None, ("leaf", "fac"), None),
        P(None, ("leaf", "fac"), None),
    )
    return jax.shard_map(
        body, mesh=mesh, in_specs=placed, out_specs=P(None, ("leaf", "fac")), check_vma=False
    )
```

```python
import functools

import jax
import jax.numpy as jnp
from jax import lax
from jax.experimental import pallas as pl
from jax.experimental.pallas import tpu as pltpu
from jax.sharding import PartitionSpec as P

CASES = 256
RANK = 128
LEVELS = 3
SLOTS = 4096
ROWS = 512
HALF = 256
WIDE = LEVELS * RANK
COPIES = 96
MESH = pl.DeviceIdType.MESH


def kernel(
    loads_ref, size_ref, order_ref, inverse_ref, left_ref, right_ref, out_ref,
    blocks, order, match, ordered, inverse, other_inverse, left, right, left_t, right_w,
    partial, from_core, field, coef, in_core, coef_core, in_y, coef_y, node, in_flip, in_near, in_zero, in_one, in_two, partner,
    mix, mix_core, mix_half, mix_near, mix_far, mix_z, mix_y, mixing, mix_split,
    local_sem, send_sem, recv_sem,
):
    leaf, fac = lax.axis_index("leaf"), lax.axis_index("fac")
    x, z = lax.div(leaf, 8), lax.rem(leaf, 8)
    y, core = lax.div(fac, 2), lax.rem(fac, 2)
    z_hi, z_lo = lax.div(z, 4), lax.rem(z, 4)
    x_pair = x + 1 - 2 * lax.rem(x, 2)
    x_far = [lax.rem(x + 2, 4), 3 - x]

    def at(x_=x, z_=z, y_=y, core_=core):
        return (x_ * 8 + z_, y_ * 2 + core_)

    def y_off(o):
        return lax.rem(y + o, 4)

    def z_off(o, flip=0):
        return lax.rem(z_hi + flip, 2) * 4 + lax.rem(z_lo + o, 4)

    def rows_of(start, count):
        return pl.ds(pl.multiple_of(start, 8), count)

    sibling = at(core_=1 - core)
    near_z = [z_off(o) for o in (1, 2, 3)]
    flip_z = [z_off(o, 1) for o in range(4)]
    z_all = [z_off(o, f) for f in range(2) for o in range(4)]
    partners = [at(y_=y_off(o)) for o in (1, 3, 2)]
    partners += [sibling]
    partners += [at(y_=y_off(o), core_=1 - core) for o in (1, 2, 3)]
    partners += [at(z_=other) for other in near_z + flip_z]
    partners += [at(x_=x_pair, z_=other) for other in z_all]
    partners += [at(x_=far, z_=other) for far in x_far for other in [z] + near_z]

    barrier = pltpu.get_barrier_semaphore()
    for other in partners:
        pl.semaphore_signal(barrier, inc=1, device_id=other, device_id_type=MESH)

    copies = []

    def send(src, dst, target):
        i = len(copies)
        copy = pltpu.make_async_remote_copy(
            src_ref=src, dst_ref=dst, send_sem=send_sem.at[i], recv_sem=recv_sem.at[i],
            device_id=target, device_id_type=MESH,
        )
        copies.append(copy)
        copy.start()
        return copy

    def recv(copy):
        copy.wait_recv()

    def fetch(i, src, dst):
        copy = pltpu.make_async_copy(src, dst, local_sem.at[i])
        copy.start()
        return copy

    got_order = fetch(1, order_ref, order)
    got_loads = fetch(0, loads_ref, blocks.at[3])
    got_left = fetch(2, left_ref, left)
    got_right = fetch(3, right_ref, right)

    pl.semaphore_wait(barrier, len(partners))

    def columns(ref, start, count):
        return ref.at[:, pl.ds(start, count)]

    up, down = at(y_=y_off(1)), at(y_=y_off(3))
    up_first = send(columns(loads_ref, 0, HALF), columns(blocks.at[0], 0, HALF), up)
    down_first = send(columns(loads_ref, HALF, HALF), columns(blocks.at[1], HALF, HALF), down)
    up_second = send(columns(loads_ref, HALF, HALF), columns(blocks.at[0], HALF, HALF), up)
    down_second = send(columns(loads_ref, 0, HALF), columns(blocks.at[1], 0, HALF), down)
    size = size_ref[0]
    first_row = fac * ROWS
    got_left.wait()
    got_right.wait()
    for level in range(LEVELS):
        live = first_row + lax.broadcasted_iota(jnp.int32, (RANK, ROWS), 1) < size
        turned = left[level].T
        left_t[level * RANK:(level + 1) * RANK, :] = jnp.where(live, turned, jnp.zeros_like(turned))
        right_w[:, level * RANK:(level + 1) * RANK] = right[level]
    mix[:, :2 * RANK] = jnp.dot(left_t[:RANK, :], right_w[:, RANK:], preferred_element_type=jnp.float32)
    mix[:, 2 * RANK:] = jnp.dot(left_t[RANK:2 * RANK, :], right_w[:, 2 * RANK:], preferred_element_type=jnp.float32)
    mix_sib = send(mix.at[rows_of(64 * (1 - core), 64), :], mix_core, sibling)

    inverse_sib = []
    for j in range(2):
        rows = pl.ds(j * HALF, HALF)
        inverse_sib.append(send(inverse_ref.at[rows, :], other_inverse.at[rows, :], sibling))
    got_inverse = fetch(4, inverse_ref, inverse)

    got_order.wait()

    place = lax.broadcasted_iota(jnp.int32, (32, 128), 0) * 128 + lax.broadcasted_iota(jnp.int32, (32, 128), 1)
    turned = jnp.where(place < size, order[...], -1).T
    for r in range(32):
        match[r * 128:(r + 1) * 128, :] = jnp.broadcast_to(turned[:, r:r + 1], (128, 128))

    owners = [y_off(3) * 2 + core, y_off(1) * 2 + core, y_off(2) * 2 + core, fac]

    def permute(parts, first=False):
        @pl.loop(0, 2)
        def _(m):
            rows = pl.ds(pl.multiple_of(m * 2048, 2048), 2048)
            slot = match[rows, :]
            total = None
            for block, start, count in parts:
                picks = []
                for j in range(count // 128):
                    here = owners[block] * ROWS + start + j * 128
                    column = here + lax.broadcasted_iota(jnp.int32, (2048, 128), 1)
                    picks.append(jnp.where(slot == column, 1.0, 0.0).astype(jnp.bfloat16))
                picks = picks[0] if len(picks) == 1 else jnp.concatenate(picks, axis=1)
                term = lax.dot_general(
                    picks, blocks[block, :, start:start + count], (((1,), (1,)), ((), ())),
                    preferred_element_type=jnp.float32,
                )
                total = term if total is None else total + term
            total = total.astype(jnp.bfloat16)
            if first:
                ordered[rows, :] = total
            else:
                ordered[rows, :] += total

    recv(mix_sib)
    mix_half[...] = mix[rows_of(64 * core, 64), :] + mix_core[...]
    to_z = []
    for o in range(4):
        rows = rows_of(16 * lax.rem(z_lo + o, 4), 16)
        to_z.append(send(mix_half.at[rows, pl.ds(0, 2 * RANK)], mix_near.at[o], at(z_=z_off(o, 1))))
        for f in range(2):
            to_z.append(send(
                mix_half.at[rows, pl.ds(2 * RANK, RANK)], mix_far.at[f * 4 + o],
                at(x_=x_pair, z_=z_off(o, f)),
            ))

    got_loads.wait()
    permute([(3, 0, ROWS)], first=True)

    forwards = []
    quarter = HALF // 2
    recv(up_first)
    for j in range(2):
        here = j * quarter
        forwards.append(send(columns(blocks.at[0], here, quarter), columns(blocks.at[2], here, quarter), up))
    recv(down_first)
    for j in range(2):
        here = HALF + (1 - j) * quarter
        forwards.append(send(columns(blocks.at[1], here, quarter), columns(blocks.at[2], here, quarter), down))
    permute([(0, 0, HALF), (1, HALF, HALF)])

    recv(up_second)
    recv(down_second)
    permute([(0, HALF, HALF), (1, 0, HALF)])

    for copy in to_z:
        recv(copy)
    mix_z[:, :2 * RANK] = mix_near[0] + mix_near[1] + mix_near[2] + mix_near[3]
    far = mix_far[0]
    for j in range(1, 8):
        far = far + mix_far[j]
    mix_z[:, 2 * RANK:] = far
    mix_across = [send(mix_z, mix_y.at[o], at(y_=y_off(o))) for o in (1, 2, 3)]

    recv(forwards[0])
    recv(forwards[2])
    permute([(2, 0, quarter), (2, 3 * quarter, quarter)])
    recv(forwards[1])
    recv(forwards[3])
    permute([(2, quarter, HALF)])

    to_core = []
    for j in range(2):
        rows = pl.ds(j * HALF, HALF)
        recv(inverse_sib[j])
        partial[rows, :] = jnp.dot(other_inverse[rows, :], ordered[...], preferred_element_type=jnp.float32)
        to_core.append(send(partial.at[rows, :], from_core.at[rows, :], sibling))

    for copy in mix_across:
        recv(copy)
    mine = rows_of(64 * core + 16 * z_lo, 16)
    mixing[mine, :] = mix_z[...] + mix_y[1] + mix_y[2] + mix_y[3]
    spread = [send(mixing.at[mine, :], mixing.at[mine, :], at(z_=other)) for other in near_z]
    got_inverse.wait()
    solved = jnp.dot(inverse[...], ordered[...], preferred_element_type=jnp.float32)
    for copy in to_core:
        recv(copy)
    live = first_row + lax.broadcasted_iota(jnp.int32, (ROWS, CASES), 0) < size
    field[...] = jnp.where(live, solved + from_core[...], 0.0).T

    def halves(value):
        high = value.astype(jnp.bfloat16)
        return high, (value - high.astype(jnp.float32)).astype(jnp.bfloat16)

    def split_dot(value, weight):
        high, low = halves(value)
        return jnp.dot(high, weight, preferred_element_type=jnp.float32) + jnp.dot(
            low, weight, preferred_element_type=jnp.float32
        )

    theirs, ours = rows_of(128 * (1 - core), 128), rows_of(128 * core, 128)
    coef[...] = split_dot(field[theirs, :], right_w[...])
    coef_sib = send(coef, in_core, sibling)
    own_coef = split_dot(field[ours, :], right_w[...])
    recv(coef_sib)
    coef_core[...] = own_coef + in_core[...]
    pair = lax.div(z_lo, 2)
    to_y = []
    for part in (1 - pair, pair):
        for o in (2, 1, 3):
            rows = rows_of(32 * y_off(o) + 16 * part, 16)
            to_y.append(send(coef_core.at[rows, :], in_y.at[o, rows_of(16 * part, 16), :], at(y_=y_off(o))))
    for copy in spread:
        recv(copy)
    sixty_four = mixing.at[rows_of(64 * core, 64), :]
    spread = send(sixty_four, sixty_four, sibling)

    def z_flip(o):
        return [z_lo, z_lo + 1 - 2 * lax.rem(z_lo, 2), lax.rem(z_lo + 2, 4), 3 - z_lo][o]

    def mixed(value, start, count):
        high, low = halves(value)
        both = jnp.concatenate([high, low], axis=0)
        by_high = jnp.dot(both, mix_split[:, start:start + count], preferred_element_type=jnp.float32)
        by_low = jnp.dot(both, mix_split[:, WIDE + start:WIDE + start + count], preferred_element_type=jnp.float32)
        return by_high[:16] + (by_high[16:] + by_low[:16])

    recv(spread)
    mix_split[:, :WIDE], mix_split[:, WIDE:] = halves(mixing[...])
    to_node = []
    for n, part in enumerate((1 - pair, pair)):
        for copy in to_y[3 * n:3 * n + 3]:
            recv(copy)
        rows = rows_of(16 * part, 16)
        summed = coef_core[rows_of(32 * y + 16 * part, 16), :] + in_y[1, rows, :] + in_y[2, rows, :] + in_y[3, rows, :]
        zero = summed[:, :RANK]
        terms = mixed(zero, 0, 2 * RANK)
        one = summed[:, RANK:2 * RANK] + terms[:, :RANK]
        two = summed[:, 2 * RANK:] + terms[:, RANK:] + mixed(one, 2 * RANK, RANK)
        coef_y[rows, :] = jnp.concatenate([zero, one, two], axis=1)
        for o in ((2, 3), (0, 1))[n]:
            eight = rows_of(8 * z_flip(o), 8)
            there = z_hi * 4 + z_flip(o)
            for g, far in enumerate(x_far):
                to_node.append(send(coef_y.at[eight, pl.ds(2 * RANK, RANK)], in_two.at[o, g], at(x_=far, z_=there)))
            to_node.append(send(coef_y.at[eight, pl.ds(RANK, RANK)], in_one.at[o], at(x_=x_pair, z_=there)))
            if o:
                to_node.append(send(coef_y.at[eight, pl.ds(0, RANK)], in_zero.at[o], at(z_=there)))
    for copy in to_node:
        recv(copy)
    node[:, :RANK] = coef_y[rows_of(8 * z_lo, 8), :RANK] + (in_zero[1] + in_zero[2] + in_zero[3])
    node[:, RANK:2 * RANK] = (in_one[0] + in_one[1]) + (in_one[2] + in_one[3])
    node[:, 2 * RANK:] = ((in_two[0, 0] + in_two[1, 0]) + (in_two[2, 0] + in_two[3, 0])) + (
        (in_two[0, 1] + in_two[1, 1]) + (in_two[2, 1] + in_two[3, 1])
    )
    over = [send(node, in_flip.at[o], at(z_=z_off(o, 1))) for o in range(4)]
    wide = pl.ds(RANK, 2 * RANK)
    over += [send(node.at[:, wide], in_near.at[o], at(z_=z_off(o))) for o in (1, 2, 3)]
    for copy in over:
        recv(copy)
    for o in range(4):
        eight = rows_of(128 * core + 32 * y + 8 * lax.rem(z_lo + 4 - o, 4), 8)
        beside = node[:, RANK:] if o == 0 else in_near[o]
        partner[eight, :RANK] = in_flip[o, :, :RANK]
        partner[eight, RANK:] = in_flip[o, :, RANK:] + beside

    def thirty_two(y_):
        return partner.at[rows_of(128 * core + 32 * y_, 32), :]

    back = [send(thirty_two(y), thirty_two(y), at(y_=y_off(o))) for o in (2, 1, 3)]
    relays = [send(thirty_two(y), thirty_two(y), at(y_=y_off(o), core_=1 - core)) for o in (2, 1, 3)]
    relays.append(send(thirty_two(y), thirty_two(y), sibling))
    for copy in back:
        recv(copy)
    out_ref[ours, :] = field[ours, :] + split_dot(partner[ours, :], left_t[...])
    for copy in relays:
        recv(copy)
    out_ref[theirs, :] = field[theirs, :] + split_dot(partner[theirs, :], left_t[...])
    for copy in copies:
        copy.wait_send()


def body(loads, leaf_sizes, tree_order, leaf_inverse, left_factors, right_factors):
    f32, bf16 = jnp.float32, jnp.bfloat16
    scratch = [
        ((4, CASES, ROWS), bf16),
        ((32, 128), jnp.int32),
        ((SLOTS, 128), jnp.int32),
        ((SLOTS, CASES), bf16),
        ((ROWS, SLOTS), bf16),
        ((ROWS, SLOTS), bf16),
        ((LEVELS, ROWS, RANK), bf16),
        ((LEVELS, ROWS, RANK), bf16),
        ((WIDE, ROWS), bf16),
        ((ROWS, WIDE), bf16),
        ((ROWS, CASES), f32),
        ((ROWS, CASES), f32),
        ((CASES, ROWS), f32),
        ((128, WIDE), f32),
        ((128, WIDE), f32),
        ((128, WIDE), f32),
        ((4, 32, WIDE), f32),
        ((32, WIDE), f32),
        ((8, WIDE), f32),
        ((4, 8, WIDE), f32),
        ((4, 8, 2 * RANK), f32),
        ((4, 8, RANK), f32),
        ((4, 8, RANK), f32),
        ((4, 2, 8, RANK), f32),
        ((CASES, WIDE), f32),
        ((RANK, WIDE), f32),
        ((64, WIDE), f32),
        ((64, WIDE), f32),
        ((4, 16, 2 * RANK), f32),
        ((8, 16, RANK), f32),
        ((16, WIDE), f32),
        ((4, 16, WIDE), f32),
        ((RANK, WIDE), f32),
        ((RANK, 2 * WIDE), bf16),
    ]
    in_hbm = pl.BlockSpec(memory_space=pltpu.HBM)
    return pl.pallas_call(
        kernel,
        out_shape=pltpu.VMEM((CASES, ROWS), f32),
        in_specs=[
            in_hbm, pl.BlockSpec(memory_space=pltpu.SMEM), in_hbm, in_hbm, in_hbm, in_hbm,
        ],
        out_specs=pl.BlockSpec(memory_space=pltpu.VMEM),
        scratch_shapes=[pltpu.VMEM(shape, dtype) for shape, dtype in scratch] + [
            pltpu.SemaphoreType.DMA((5,)),
            pltpu.SemaphoreType.DMA((COPIES,)),
            pltpu.SemaphoreType.DMA((COPIES,)),
        ],
        compiler_params=pltpu.CompilerParams(
            collective_id=0, has_side_effects=True, vmem_limit_bytes=60 << 20
        ),
    )(loads, leaf_sizes, tree_order.reshape(32, 128), leaf_inverse, left_factors, right_factors)


def solution(mesh):
    placed = (
        P(None, ("leaf", "fac")),
        P("leaf"),
        P("leaf", None),
        P(("leaf", "fac"), None),
        P(None, ("leaf", "fac"), None),
        P(None, ("leaf", "fac"), None),
    )
    return jax.shard_map(
        body, mesh=mesh, in_specs=placed, out_specs=P(None, ("leaf", "fac")), check_vma=False
    )
```

```python
import functools

import jax
import jax.numpy as jnp
from jax import lax
from jax.experimental import pallas as pl
from jax.experimental.pallas import tpu as pltpu
from jax.sharding import PartitionSpec as P

CASES = 256
RANK = 128
LEVELS = 3
SLOTS = 4096
ROWS = 512
HALF = 256
WIDE = LEVELS * RANK
COPIES = 96
MESH = pl.DeviceIdType.MESH


def kernel(
    loads_ref, size_ref, order_ref, inverse_ref, left_ref, right_ref, out_ref,
    blocks, order, match, ordered, inverse, left, right, left_t, right_w,
    partial, from_core, field, coef_core, in_y, coef_y, node, in_flip, in_near,
    in_zero, in_one, in_two, partner, out_far,
    mix, mix_core, mix_half, mix_near, mix_far, mix_z, mix_y, mixing, mix_split,
    local_sem, send_sem, recv_sem,
):
    leaf, fac = lax.axis_index("leaf"), lax.axis_index("fac")
    x, z = lax.div(leaf, 8), lax.rem(leaf, 8)
    y, core = lax.div(fac, 2), lax.rem(fac, 2)
    z_hi, z_lo = lax.div(z, 4), lax.rem(z, 4)
    x_pair = x + 1 - 2 * lax.rem(x, 2)
    x_far = [lax.rem(x + 2, 4), 3 - x]

    def at(x_=x, z_=z, y_=y, core_=core):
        return (x_ * 8 + z_, y_ * 2 + core_)

    def y_off(o):
        return lax.rem(y + o, 4)

    def z_off(o, flip=0):
        return lax.rem(z_hi + flip, 2) * 4 + lax.rem(z_lo + o, 4)

    def rows_of(start, count):
        return pl.ds(pl.multiple_of(start, 8), count)

    sibling = at(core_=1 - core)
    near_z = [z_off(o) for o in (1, 2, 3)]
    flip_z = [z_off(o, 1) for o in range(4)]
    z_all = [z_off(o, f) for f in range(2) for o in range(4)]
    partners = [at(y_=y_off(o)) for o in (1, 3, 2)]
    partners += [sibling]
    partners += [at(z_=other) for other in near_z + flip_z]
    partners += [at(x_=x_pair, z_=other) for other in z_all]
    partners += [at(x_=far, z_=other) for far in x_far for other in [z] + near_z]

    barrier = pltpu.get_barrier_semaphore()
    for other in partners:
        pl.semaphore_signal(barrier, inc=1, device_id=other, device_id_type=MESH)

    copies = []

    def send(src, dst, target):
        i = len(copies)
        copy = pltpu.make_async_remote_copy(
            src_ref=src, dst_ref=dst, send_sem=send_sem.at[i], recv_sem=recv_sem.at[i],
            device_id=target, device_id_type=MESH,
        )
        copies.append(copy)
        copy.start()
        return copy

    def recv(copy):
        copy.wait_recv()

    def fetch(i, src, dst):
        copy = pltpu.make_async_copy(src, dst, local_sem.at[i])
        copy.start()
        return copy

    got_order = fetch(1, order_ref, order)
    got_loads = fetch(0, loads_ref, blocks.at[3])
    got_left = fetch(2, left_ref, left)
    got_right = fetch(3, right_ref, right)

    pl.semaphore_wait(barrier, len(partners))

    def columns(ref, start, count):
        return ref.at[:, pl.ds(start, count)]

    up, down = at(y_=y_off(1)), at(y_=y_off(3))
    up_first = send(columns(loads_ref, 0, HALF), columns(blocks.at[0], 0, HALF), up)
    down_first = send(columns(loads_ref, HALF, HALF), columns(blocks.at[1], HALF, HALF), down)
    up_second = send(columns(loads_ref, HALF, HALF), columns(blocks.at[0], HALF, HALF), up)
    down_second = send(columns(loads_ref, 0, HALF), columns(blocks.at[1], 0, HALF), down)
    size = size_ref[0]
    first_row = fac * ROWS
    got_left.wait()
    got_right.wait()
    for level in range(LEVELS):
        live = first_row + lax.broadcasted_iota(jnp.int32, (RANK, ROWS), 1) < size
        turned = left[level].T
        left_t[core, level * RANK:(level + 1) * RANK, :] = jnp.where(live, turned, jnp.zeros_like(turned))
        right_w[core, :, level * RANK:(level + 1) * RANK] = right[level]
    mix[:, :2 * RANK] = jnp.dot(left_t[core, :RANK, :], right_w[core, :, RANK:], preferred_element_type=jnp.float32)
    mix[:, 2 * RANK:] = jnp.dot(
        left_t[core, RANK:2 * RANK, :], right_w[core, :, 2 * RANK:], preferred_element_type=jnp.float32
    )
    mix_sib = send(mix.at[rows_of(64 * (1 - core), 64), :], mix_core, sibling)

    inverse_sib = send(inverse_ref, inverse.at[core], sibling)
    right_sib = send(right_w.at[core], right_w.at[core], sibling)
    left_sib = send(left_t.at[core], left_t.at[core], sibling)
    got_inverse = fetch(4, inverse_ref, inverse.at[core])

    got_order.wait()

    place = lax.broadcasted_iota(jnp.int32, (32, 128), 0) * 128 + lax.broadcasted_iota(jnp.int32, (32, 128), 1)
    turned = jnp.where(place < size, order[...], -1).T
    for r in range(32):
        match[r * 128:(r + 1) * 128, :] = jnp.broadcast_to(turned[:, r:r + 1], (128, 128))

    owners = [y_off(3) * 2 + core, y_off(1) * 2 + core, y_off(2) * 2 + core, fac]

    def permute(parts, first=False, tall=2048):
        @pl.loop(0, SLOTS // tall)
        def _(m):
            rows = pl.ds(pl.multiple_of(m * tall, tall), tall)
            slot = match[rows, :]
            picks, held = [], []
            for block, start, count in parts:
                held.append(blocks[block, :, start:start + count])
                for j in range(count // 128):
                    here = owners[block] * ROWS + start + j * 128
                    column = here + lax.broadcasted_iota(jnp.int32, (tall, 128), 1)
                    picks.append(jnp.where(slot == column, 1.0, 0.0).astype(jnp.bfloat16))
            held = held[0] if len(held) == 1 else jnp.concatenate(held, axis=1)
            total = lax.dot_general(
                jnp.concatenate(picks, axis=1), held, (((1,), (1,)), ((), ())),
                preferred_element_type=jnp.float32,
            )
            total = total.astype(jnp.bfloat16)
            if first:
                ordered[rows, :] = total
            else:
                ordered[rows, :] += total

    recv(mix_sib)
    mix_half[...] = mix[rows_of(64 * core, 64), :] + mix_core[...]
    to_z = []
    for o in range(4):
        rows = rows_of(16 * lax.rem(z_lo + o, 4), 16)
        to_z.append(send(mix_half.at[rows, pl.ds(0, 2 * RANK)], mix_near.at[o], at(z_=z_off(o, 1))))
        for f in range(2):
            to_z.append(send(
                mix_half.at[rows, pl.ds(2 * RANK, RANK)], mix_far.at[f * 4 + o],
                at(x_=x_pair, z_=z_off(o, f)),
            ))

    got_loads.wait()
    permute([(3, 0, ROWS)], first=True)

    forwards = []
    quarter = HALF // 2
    recv(up_first)
    for j in range(2):
        here = j * quarter
        forwards.append(send(columns(blocks.at[0], here, quarter), columns(blocks.at[2], here, quarter), up))
    recv(down_first)
    for j in range(2):
        here = HALF + (1 - j) * quarter
        forwards.append(send(columns(blocks.at[1], here, quarter), columns(blocks.at[2], here, quarter), down))
    permute([(0, 0, HALF), (1, HALF, HALF)])

    recv(up_second)
    recv(down_second)
    permute([(0, HALF, HALF), (1, 0, HALF)])

    for copy in to_z:
        recv(copy)
    mix_z[:, :2 * RANK] = mix_near[0] + mix_near[1] + mix_near[2] + mix_near[3]
    far = mix_far[0]
    for j in range(1, 8):
        far = far + mix_far[j]
    mix_z[:, 2 * RANK:] = far
    mix_across = [send(mix_z, mix_y.at[o], at(y_=y_off(o))) for o in (1, 2, 3)]

    recv(forwards[0])
    recv(forwards[2])
    permute([(2, 0, quarter), (2, 3 * quarter, quarter)])
    recv(forwards[1])
    recv(forwards[3])
    permute([(2, quarter, HALF)])

    got_inverse.wait()
    recv(inverse_sib)
    to_core = []

    def solve(b, start, count):
        rows = pl.ds(start, count)
        solved = jnp.dot(inverse[b, rows, :], ordered[...], preferred_element_type=jnp.float32)
        for h in range(2):
            partial[h, b, rows, :] = solved[:, 128 * h:128 * h + 128]
        to_core.append(send(partial.at[1 - core, b, rows, :], from_core.at[b, rows, :], sibling))

    solve(0, 0, ROWS)
    solve(1, 0, ROWS)
    for copy in mix_across:
        recv(copy)
    mine = rows_of(64 * core + 16 * z_lo, 16)
    mixing[mine, :] = mix_z[...] + mix_y[1] + mix_y[2] + mix_y[3]
    spread = [send(mixing.at[mine, :], mixing.at[mine, :], at(z_=other)) for other in near_z]

    def settle(b):
        live = y * 2 * ROWS + b * ROWS + lax.broadcasted_iota(jnp.int32, (ROWS, 128), 0) < size
        field[b] = jnp.where(live, partial[core, b] + from_core[b], 0.0).T

    def halves(value):
        high = value.astype(jnp.bfloat16)
        return high, (value - high.astype(jnp.float32)).astype(jnp.bfloat16)

    def split_dot(value, weight):
        high, low = halves(value)
        return jnp.dot(high, weight, preferred_element_type=jnp.float32) + jnp.dot(
            low, weight, preferred_element_type=jnp.float32
        )

    recv(to_core[0])
    recv(right_sib)
    settle(0)
    early = split_dot(field[0], right_w[0])
    recv(to_core[1])
    settle(1)
    coef_core[...] = early + split_dot(field[1], right_w[1])
    pair = lax.div(z_lo, 2)
    to_y = []
    for part in (1 - pair, pair):
        for o in (2, 1, 3):
            rows = rows_of(32 * y_off(o) + 16 * part, 16)
            to_y.append(send(coef_core.at[rows, :], in_y.at[o, rows_of(16 * part, 16), :], at(y_=y_off(o))))
    for copy in spread:
        recv(copy)
    sixty_four = mixing.at[rows_of(64 * core, 64), :]
    spread = send(sixty_four, sixty_four, sibling)

    def z_flip(o):
        return [z_lo, z_lo + 1 - 2 * lax.rem(z_lo, 2), lax.rem(z_lo + 2, 4), 3 - z_lo][o]

    def mixed(value, start, count):
        high, low = halves(value)
        both = jnp.concatenate([high, low], axis=0)
        by_high = jnp.dot(both, mix_split[:, start:start + count], preferred_element_type=jnp.float32)
        by_low = jnp.dot(both, mix_split[:, WIDE + start:WIDE + start + count], preferred_element_type=jnp.float32)
        return by_high[:16] + (by_high[16:] + by_low[:16])

    recv(spread)
    mix_split[:, :WIDE], mix_split[:, WIDE:] = halves(mixing[...])
    to_node = []
    for n, part in enumerate((1 - pair, pair)):
        for copy in to_y[3 * n:3 * n + 3]:
            recv(copy)
        rows = rows_of(16 * part, 16)
        summed = coef_core[rows_of(32 * y + 16 * part, 16), :] + in_y[1, rows, :] + in_y[2, rows, :] + in_y[3, rows, :]
        zero = summed[:, :RANK]
        terms = mixed(zero, 0, 2 * RANK)
        one = summed[:, RANK:2 * RANK] + terms[:, :RANK]
        two = summed[:, 2 * RANK:] + terms[:, RANK:] + mixed(one, 2 * RANK, RANK)
        coef_y[rows, :] = jnp.concatenate([zero, one, two], axis=1)
        for o in ((2, 3), (0, 1))[n]:
            eight = rows_of(8 * z_flip(o), 8)
            there = z_hi * 4 + z_flip(o)
            for g, far in enumerate(x_far):
                to_node.append(send(coef_y.at[eight, pl.ds(2 * RANK, RANK)], in_two.at[o, g], at(x_=far, z_=there)))
            to_node.append(send(coef_y.at[eight, pl.ds(RANK, RANK)], in_one.at[o], at(x_=x_pair, z_=there)))
            if o:
                to_node.append(send(coef_y.at[eight, pl.ds(0, RANK)], in_zero.at[o], at(z_=there)))
    for copy in to_node:
        recv(copy)
    node[:, :RANK] = coef_y[rows_of(8 * z_lo, 8), :RANK] + (in_zero[1] + in_zero[2] + in_zero[3])
    node[:, RANK:2 * RANK] = (in_one[0] + in_one[1]) + (in_one[2] + in_one[3])
    node[:, 2 * RANK:] = ((in_two[0, 0] + in_two[1, 0]) + (in_two[2, 0] + in_two[3, 0])) + (
        (in_two[0, 1] + in_two[1, 1]) + (in_two[2, 1] + in_two[3, 1])
    )
    over = [send(node, in_flip.at[o], at(z_=z_off(o, 1))) for o in range(4)]
    wide = pl.ds(RANK, 2 * RANK)
    over += [send(node.at[:, wide], in_near.at[o], at(z_=z_off(o))) for o in (1, 2, 3)]
    for copy in over:
        recv(copy)
    for o in range(4):
        eight = rows_of(32 * y + 8 * lax.rem(z_lo + 4 - o, 4), 8)
        beside = node[:, RANK:] if o == 0 else in_near[o]
        partner[eight, :RANK] = in_flip[o, :, :RANK]
        partner[eight, RANK:] = in_flip[o, :, RANK:] + beside

    thirty_two = partner.at[rows_of(32 * y, 32), :]
    back = [send(thirty_two, thirty_two, at(y_=y_off(o))) for o in (2, 1, 3)]
    recv(left_sib)
    for copy in back:
        recv(copy)
    ours = rows_of(128 * core, 128)
    out_far[...] = field[1 - core] + split_dot(partner[...], left_t[1 - core])
    to_out = send(out_far, out_ref.at[ours, :], sibling)
    out_ref[ours, :] = field[core] + split_dot(partner[...], left_t[core])
    recv(to_out)
    for copy in copies:
        copy.wait_send()


def body(loads, leaf_sizes, tree_order, leaf_inverse, left_factors, right_factors):
    f32, bf16 = jnp.float32, jnp.bfloat16
    scratch = [
        ((4, CASES, ROWS), bf16),
        ((32, 128), jnp.int32),
        ((SLOTS, 128), jnp.int32),
        ((SLOTS, CASES), bf16),
        ((2, ROWS, SLOTS), bf16),
        ((LEVELS, ROWS, RANK), bf16),
        ((LEVELS, ROWS, RANK), bf16),
        ((2, WIDE, ROWS), bf16),
        ((2, ROWS, WIDE), bf16),
        ((2, 2, ROWS, 128), f32),
        ((2, ROWS, 128), f32),
        ((2, 128, ROWS), f32),
        ((128, WIDE), f32),
        ((4, 32, WIDE), f32),
        ((32, WIDE), f32),
        ((8, WIDE), f32),
        ((4, 8, WIDE), f32),
        ((4, 8, 2 * RANK), f32),
        ((4, 8, RANK), f32),
        ((4, 8, RANK), f32),
        ((4, 2, 8, RANK), f32),
        ((128, WIDE), f32),
        ((128, ROWS), f32),
        ((RANK, WIDE), f32),
        ((64, WIDE), f32),
        ((64, WIDE), f32),
        ((4, 16, 2 * RANK), f32),
        ((8, 16, RANK), f32),
        ((16, WIDE), f32),
        ((4, 16, WIDE), f32),
        ((RANK, WIDE), f32),
        ((RANK, 2 * WIDE), bf16),
    ]
    in_hbm = pl.BlockSpec(memory_space=pltpu.HBM)
    return pl.pallas_call(
        kernel,
        out_shape=pltpu.VMEM((CASES, ROWS), f32),
        in_specs=[
            in_hbm, pl.BlockSpec(memory_space=pltpu.SMEM), in_hbm, in_hbm, in_hbm, in_hbm,
        ],
        out_specs=pl.BlockSpec(memory_space=pltpu.VMEM),
        scratch_shapes=[pltpu.VMEM(shape, dtype) for shape, dtype in scratch] + [
            pltpu.SemaphoreType.DMA((5,)),
            pltpu.SemaphoreType.DMA((COPIES,)),
            pltpu.SemaphoreType.DMA((COPIES,)),
        ],
        compiler_params=pltpu.CompilerParams(
            collective_id=0, has_side_effects=True, vmem_limit_bytes=60 << 20
        ),
    )(loads, leaf_sizes, tree_order.reshape(32, 128), leaf_inverse, left_factors, right_factors)


def solution(mesh):
    placed = (
        P(None, ("leaf", "fac")),
        P("leaf"),
        P("leaf", None),
        P(("leaf", "fac"), None),
        P(None, ("leaf", "fac"), None),
        P(None, ("leaf", "fac"), None),
    )
    return jax.shard_map(
        body, mesh=mesh, in_specs=placed, out_specs=P(None, ("leaf", "fac")), check_vma=False
    )
```

```python
import functools

import jax
import jax.numpy as jnp
from jax import lax
from jax.experimental import pallas as pl
from jax.experimental.pallas import tpu as pltpu
from jax.sharding import PartitionSpec as P

CASES = 256
RANK = 128
LEVELS = 3
SLOTS = 4096
ROWS = 512
HALF = 256
WIDE = LEVELS * RANK
COPIES = 96
MESH = pl.DeviceIdType.MESH


def kernel(
    loads_ref, size_ref, order_ref, inverse_ref, left_ref, right_ref, out_ref,
    blocks, order, match, ordered, inverse, left, right, left_t, right_w,
    partial, from_core, field, coef_core, in_y, coef_y, node, in_flip, in_near,
    in_zero, in_one, in_two, partner, out_far,
    mix, mix_core, mix_half, mix_near, mix_far, mix_z, mix_y, mixing, mix_split,
    local_sem, send_sem, recv_sem,
):
    leaf, fac = lax.axis_index("leaf"), lax.axis_index("fac")
    x, z = lax.div(leaf, 8), lax.rem(leaf, 8)
    y, core = lax.div(fac, 2), lax.rem(fac, 2)
    z_hi, z_lo = lax.div(z, 4), lax.rem(z, 4)
    x_pair = x + 1 - 2 * lax.rem(x, 2)
    x_far = [lax.rem(x + 2, 4), 3 - x]

    def at(x_=x, z_=z, y_=y, core_=core):
        return (x_ * 8 + z_, y_ * 2 + core_)

    def y_off(o):
        return lax.rem(y + o, 4)

    def z_off(o, flip=0):
        return lax.rem(z_hi + flip, 2) * 4 + lax.rem(z_lo + o, 4)

    def rows_of(start, count):
        return pl.ds(pl.multiple_of(start, 8), count)

    sibling = at(core_=1 - core)
    near_z = [z_off(o) for o in (1, 2, 3)]
    flip_z = [z_off(o, 1) for o in range(4)]
    z_all = [z_off(o, f) for f in range(2) for o in range(4)]
    partners = [at(y_=y_off(o)) for o in (1, 3, 2)]
    partners += [sibling]
    partners += [at(z_=other) for other in near_z + flip_z]
    partners += [at(x_=x_pair, z_=other) for other in z_all]
    partners += [at(x_=far, z_=other) for far in x_far for other in [z] + near_z]

    barrier = pltpu.get_barrier_semaphore()
    for other in partners:
        pl.semaphore_signal(barrier, inc=1, device_id=other, device_id_type=MESH)

    copies = []

    def send(src, dst, target):
        i = len(copies)
        copy = pltpu.make_async_remote_copy(
            src_ref=src, dst_ref=dst, send_sem=send_sem.at[i], recv_sem=recv_sem.at[i],
            device_id=target, device_id_type=MESH,
        )
        copies.append(copy)
        copy.start()
        return copy

    def recv(copy):
        copy.wait_recv()

    def fetch(i, src, dst):
        copy = pltpu.make_async_copy(src, dst, local_sem.at[i])
        copy.start()
        return copy

    got_order = fetch(1, order_ref, order)
    got_loads = fetch(0, loads_ref, blocks.at[3])
    got_left = fetch(2, left_ref, left)
    got_right = fetch(3, right_ref, right)

    pl.semaphore_wait(barrier, len(partners))

    def columns(ref, start, count):
        return ref.at[:, pl.ds(start, count)]

    up, down = at(y_=y_off(1)), at(y_=y_off(3))
    up_first = send(columns(loads_ref, 0, HALF), columns(blocks.at[0], 0, HALF), up)
    down_first = send(columns(loads_ref, HALF, HALF), columns(blocks.at[1], HALF, HALF), down)
    up_second = send(columns(loads_ref, HALF, HALF), columns(blocks.at[0], HALF, HALF), up)
    down_second = send(columns(loads_ref, 0, HALF), columns(blocks.at[1], 0, HALF), down)
    size = size_ref[0]
    first_row = fac * ROWS
    got_left.wait()
    got_right.wait()
    for level in range(LEVELS):
        live = first_row + lax.broadcasted_iota(jnp.int32, (RANK, ROWS), 1) < size
        turned = left[level].T
        left_t[core, level * RANK:(level + 1) * RANK, :] = jnp.where(live, turned, jnp.zeros_like(turned))
        right_w[core, :, level * RANK:(level + 1) * RANK] = right[level]
    mix[:, :2 * RANK] = jnp.dot(left_t[core, :RANK, :], right_w[core, :, RANK:], preferred_element_type=jnp.float32)
    mix[:, 2 * RANK:] = jnp.dot(
        left_t[core, RANK:2 * RANK, :], right_w[core, :, 2 * RANK:], preferred_element_type=jnp.float32
    )
    mix_sib = send(mix.at[rows_of(64 * (1 - core), 64), :], mix_core, sibling)

    inverse_sib = send(inverse_ref, inverse.at[core], sibling)
    right_sib = send(right_w.at[core], right_w.at[core], sibling)
    left_sib = send(left_t.at[core], left_t.at[core], sibling)
    got_inverse = fetch(4, inverse_ref, inverse.at[core])

    got_order.wait()

    place = lax.broadcasted_iota(jnp.int32, (32, 128), 0) * 128 + lax.broadcasted_iota(jnp.int32, (32, 128), 1)
    turned = jnp.where(place < size, order[...], -1).T
    for r in range(32):
        match[r * 128:(r + 1) * 128, :] = jnp.broadcast_to(turned[:, r:r + 1], (128, 128))

    owners = [y_off(3) * 2 + core, y_off(1) * 2 + core, y_off(2) * 2 + core, fac]

    def permute(parts, first=False, tall=2048):
        @pl.loop(0, SLOTS // tall)
        def _(m):
            rows = pl.ds(pl.multiple_of(m * tall, tall), tall)
            slot = match[rows, :]
            picks, held = [], []
            for block, start, count in parts:
                held.append(blocks[block, :, start:start + count])
                for j in range(count // 128):
                    here = owners[block] * ROWS + start + j * 128
                    column = here + lax.broadcasted_iota(jnp.int32, (tall, 128), 1)
                    picks.append(jnp.where(slot == column, 1.0, 0.0).astype(jnp.bfloat16))
            held = held[0] if len(held) == 1 else jnp.concatenate(held, axis=1)
            total = lax.dot_general(
                jnp.concatenate(picks, axis=1), held, (((1,), (1,)), ((), ())),
                preferred_element_type=jnp.float32,
            )
            total = total.astype(jnp.bfloat16)
            if first:
                ordered[rows, :] = total
            else:
                ordered[rows, :] += total

    recv(mix_sib)
    mix_half[...] = mix[rows_of(64 * core, 64), :] + mix_core[...]
    to_z = []
    for o in range(4):
        rows = rows_of(16 * lax.rem(z_lo + o, 4), 16)
        to_z.append(send(mix_half.at[rows, pl.ds(0, 2 * RANK)], mix_near.at[o], at(z_=z_off(o, 1))))
        for f in range(2):
            to_z.append(send(
                mix_half.at[rows, pl.ds(2 * RANK, RANK)], mix_far.at[f * 4 + o],
                at(x_=x_pair, z_=z_off(o, f)),
            ))

    got_loads.wait()
    permute([(3, 0, ROWS)], first=True)

    forwards = []
    quarter = HALF // 2
    recv(up_first)
    for j in range(2):
        here = j * quarter
        forwards.append(send(columns(blocks.at[0], here, quarter), columns(blocks.at[2], here, quarter), up))
    recv(down_first)
    for j in range(2):
        here = HALF + (1 - j) * quarter
        forwards.append(send(columns(blocks.at[1], here, quarter), columns(blocks.at[2], here, quarter), down))
    permute([(0, 0, HALF), (1, HALF, HALF)])

    recv(up_second)
    recv(down_second)
    permute([(0, HALF, HALF), (1, 0, HALF)])

    for copy in to_z:
        recv(copy)
    mix_z[:, :2 * RANK] = mix_near[0] + mix_near[1] + mix_near[2] + mix_near[3]
    far = mix_far[0]
    for j in range(1, 8):
        far = far + mix_far[j]
    mix_z[:, 2 * RANK:] = far
    mix_across = [send(mix_z, mix_y.at[o], at(y_=y_off(o))) for o in (1, 2, 3)]

    recv(forwards[0])
    recv(forwards[2])
    recv(forwards[1])
    recv(forwards[3])
    permute([(2, 0, ROWS)])

    got_inverse.wait()
    recv(inverse_sib)
    base = len(copies)

    def swap(b):
        return pltpu.make_async_remote_copy(
            src_ref=partial.at[1 - core, b], dst_ref=from_core.at[b], send_sem=send_sem.at[base + b],
            recv_sem=recv_sem.at[base + b], device_id=sibling, device_id_type=MESH,
        )

    @pl.loop(0, 2)
    def _(b):
        solved = jnp.dot(inverse[b], ordered[...], preferred_element_type=jnp.float32)
        for h in range(2):
            partial[h, b] = solved[:, 128 * h:128 * h + 128]
        swap(b).start()

    to_core = [swap(0), swap(1)]
    copies += to_core
    for copy in mix_across:
        recv(copy)
    mine = rows_of(64 * core + 16 * z_lo, 16)
    mixing[mine, :] = mix_z[...] + mix_y[1] + mix_y[2] + mix_y[3]
    spread = [send(mixing.at[mine, :], mixing.at[mine, :], at(z_=other)) for other in near_z]

    def settle(b):
        live = y * 2 * ROWS + b * ROWS + lax.broadcasted_iota(jnp.int32, (ROWS, 128), 0) < size
        field[b] = jnp.where(live, partial[core, b] + from_core[b], 0.0).T

    def halves(value):
        high = value.astype(jnp.bfloat16)
        return high, (value - high.astype(jnp.float32)).astype(jnp.bfloat16)

    def split_dot(value, weight):
        high, low = halves(value)
        return jnp.dot(high, weight, preferred_element_type=jnp.float32) + jnp.dot(
            low, weight, preferred_element_type=jnp.float32
        )

    recv(to_core[0])
    recv(right_sib)
    settle(0)
    early = split_dot(field[0], right_w[0])
    recv(to_core[1])
    settle(1)
    coef_core[...] = early + split_dot(field[1], right_w[1])
    pair = lax.div(z_lo, 2)
    to_y = []
    for part in (1 - pair, pair):
        for o in (2, 1, 3):
            rows = rows_of(32 * y_off(o) + 16 * part, 16)
            to_y.append(send(coef_core.at[rows, :], in_y.at[o, rows_of(16 * part, 16), :], at(y_=y_off(o))))
    for copy in spread:
        recv(copy)
    sixty_four = mixing.at[rows_of(64 * core, 64), :]
    spread = send(sixty_four, sixty_four, sibling)

    def z_flip(o):
        return [z_lo, z_lo + 1 - 2 * lax.rem(z_lo, 2), lax.rem(z_lo + 2, 4), 3 - z_lo][o]

    def mixed(value, start, count):
        high, low = halves(value)
        both = jnp.concatenate([high, low], axis=0)
        by_high = jnp.dot(both, mix_split[:, start:start + count], preferred_element_type=jnp.float32)
        by_low = jnp.dot(both, mix_split[:, WIDE + start:WIDE + start + count], preferred_element_type=jnp.float32)
        return by_high[:16] + (by_high[16:] + by_low[:16])

    recv(spread)
    mix_split[:, :WIDE], mix_split[:, WIDE:] = halves(mixing[...])
    to_node = []
    for n, part in enumerate((1 - pair, pair)):
        for copy in to_y[3 * n:3 * n + 3]:
            recv(copy)
        rows = rows_of(16 * part, 16)
        summed = coef_core[rows_of(32 * y + 16 * part, 16), :] + in_y[1, rows, :] + in_y[2, rows, :] + in_y[3, rows, :]
        zero = summed[:, :RANK]
        terms = mixed(zero, 0, 2 * RANK)
        one = summed[:, RANK:2 * RANK] + terms[:, :RANK]
        two = summed[:, 2 * RANK:] + terms[:, RANK:] + mixed(one, 2 * RANK, RANK)
        coef_y[rows, :] = jnp.concatenate([zero, one, two], axis=1)
        for o in ((2, 3), (0, 1))[n]:
            eight = rows_of(8 * z_flip(o), 8)
            there = z_hi * 4 + z_flip(o)
            for g, far in enumerate(x_far):
                to_node.append(send(coef_y.at[eight, pl.ds(2 * RANK, RANK)], in_two.at[o, g], at(x_=far, z_=there)))
            to_node.append(send(coef_y.at[eight, pl.ds(RANK, RANK)], in_one.at[o], at(x_=x_pair, z_=there)))
            if o:
                to_node.append(send(coef_y.at[eight, pl.ds(0, RANK)], in_zero.at[o], at(z_=there)))
    for copy in to_node:
        recv(copy)
    node[:, :RANK] = coef_y[rows_of(8 * z_lo, 8), :RANK] + (in_zero[1] + in_zero[2] + in_zero[3])
    node[:, RANK:2 * RANK] = (in_one[0] + in_one[1]) + (in_one[2] + in_one[3])
    node[:, 2 * RANK:] = ((in_two[0, 0] + in_two[1, 0]) + (in_two[2, 0] + in_two[3, 0])) + (
        (in_two[0, 1] + in_two[1, 1]) + (in_two[2, 1] + in_two[3, 1])
    )
    over = [send(node, in_flip.at[o], at(z_=z_off(o, 1))) for o in range(4)]
    wide = pl.ds(RANK, 2 * RANK)
    over += [send(node.at[:, wide], in_near.at[o], at(z_=z_off(o))) for o in (1, 2, 3)]
    for copy in over:
        recv(copy)
    for o in range(4):
        eight = rows_of(32 * y + 8 * lax.rem(z_lo + 4 - o, 4), 8)
        beside = node[:, RANK:] if o == 0 else in_near[o]
        partner[eight, :RANK] = in_flip[o, :, :RANK]
        partner[eight, RANK:] = in_flip[o, :, RANK:] + beside

    thirty_two = partner.at[rows_of(32 * y, 32), :]
    back = [send(thirty_two, thirty_two, at(y_=y_off(o))) for o in (2, 1, 3)]
    recv(left_sib)
    for copy in back:
        recv(copy)
    ours = rows_of(128 * core, 128)
    out_far[...] = field[1 - core] + split_dot(partner[...], left_t[1 - core])
    to_out = send(out_far, out_ref.at[ours, :], sibling)
    out_ref[ours, :] = field[core] + split_dot(partner[...], left_t[core])
    recv(to_out)
    for copy in copies:
        copy.wait_send()


def body(loads, leaf_sizes, tree_order, leaf_inverse, left_factors, right_factors):
    f32, bf16 = jnp.float32, jnp.bfloat16
    scratch = [
        ((4, CASES, ROWS), bf16),
        ((32, 128), jnp.int32),
        ((SLOTS, 128), jnp.int32),
        ((SLOTS, CASES), bf16),
        ((2, ROWS, SLOTS), bf16),
        ((LEVELS, ROWS, RANK), bf16),
        ((LEVELS, ROWS, RANK), bf16),
        ((2, WIDE, ROWS), bf16),
        ((2, ROWS, WIDE), bf16),
        ((2, 2, ROWS, 128), f32),
        ((2, ROWS, 128), f32),
        ((2, 128, ROWS), f32),
        ((128, WIDE), f32),
        ((4, 32, WIDE), f32),
        ((32, WIDE), f32),
        ((8, WIDE), f32),
        ((4, 8, WIDE), f32),
        ((4, 8, 2 * RANK), f32),
        ((4, 8, RANK), f32),
        ((4, 8, RANK), f32),
        ((4, 2, 8, RANK), f32),
        ((128, WIDE), f32),
        ((128, ROWS), f32),
        ((RANK, WIDE), f32),
        ((64, WIDE), f32),
        ((64, WIDE), f32),
        ((4, 16, 2 * RANK), f32),
        ((8, 16, RANK), f32),
        ((16, WIDE), f32),
        ((4, 16, WIDE), f32),
        ((RANK, WIDE), f32),
        ((RANK, 2 * WIDE), bf16),
    ]
    in_hbm = pl.BlockSpec(memory_space=pltpu.HBM)
    return pl.pallas_call(
        kernel,
        out_shape=pltpu.VMEM((CASES, ROWS), f32),
        in_specs=[
            in_hbm, pl.BlockSpec(memory_space=pltpu.SMEM), in_hbm, in_hbm, in_hbm, in_hbm,
        ],
        out_specs=pl.BlockSpec(memory_space=pltpu.VMEM),
        scratch_shapes=[pltpu.VMEM(shape, dtype) for shape, dtype in scratch] + [
            pltpu.SemaphoreType.DMA((5,)),
            pltpu.SemaphoreType.DMA((COPIES,)),
            pltpu.SemaphoreType.DMA((COPIES,)),
        ],
        compiler_params=pltpu.CompilerParams(
            collective_id=0, has_side_effects=True, vmem_limit_bytes=60 << 20
        ),
    )(loads, leaf_sizes, tree_order.reshape(32, 128), leaf_inverse, left_factors, right_factors)


def solution(mesh):
    placed = (
        P(None, ("leaf", "fac")),
        P("leaf"),
        P("leaf", None),
        P(("leaf", "fac"), None),
        P(None, ("leaf", "fac"), None),
        P(None, ("leaf", "fac"), None),
    )
    return jax.shard_map(
        body, mesh=mesh, in_specs=placed, out_specs=P(None, ("leaf", "fac")), check_vma=False
    )
```

```python
import functools

import jax
import jax.numpy as jnp
from jax import lax
from jax.experimental import pallas as pl
from jax.experimental.pallas import tpu as pltpu
from jax.sharding import PartitionSpec as P

CASES = 256
RANK = 128
LEVELS = 3
SLOTS = 4096
ROWS = 512
HALF = 256
WIDE = LEVELS * RANK
COPIES = 96
MESH = pl.DeviceIdType.MESH


def kernel(
    loads_ref, size_ref, order_ref, inverse_ref, left_ref, right_ref, out_ref,
    blocks, order, match, ordered, inverse, left, right, left_t, right_w,
    partial, from_core, field, coef_core, in_y, coef_y, node, in_flip, in_near,
    in_zero, in_one, in_two, partner, out_far,
    mix, mix_core, mix_half, mix_near, mix_far, mix_z, mix_y, mixing, mix_split,
    local_sem, send_sem, recv_sem,
):
    leaf, fac = lax.axis_index("leaf"), lax.axis_index("fac")
    x, z = lax.div(leaf, 8), lax.rem(leaf, 8)
    y, core = lax.div(fac, 2), lax.rem(fac, 2)
    z_hi, z_lo = lax.div(z, 4), lax.rem(z, 4)
    x_pair = x + 1 - 2 * lax.rem(x, 2)
    x_far = [lax.rem(x + 2, 4), 3 - x]

    def at(x_=x, z_=z, y_=y, core_=core):
        return (x_ * 8 + z_, y_ * 2 + core_)

    def y_off(o):
        return lax.rem(y + o, 4)

    def z_off(o, flip=0):
        return lax.rem(z_hi + flip, 2) * 4 + lax.rem(z_lo + o, 4)

    def rows_of(start, count):
        return pl.ds(pl.multiple_of(start, 8), count)

    sibling = at(core_=1 - core)
    near_z = [z_off(o) for o in (1, 2, 3)]
    flip_z = [z_off(o, 1) for o in range(4)]
    z_all = [z_off(o, f) for f in range(2) for o in range(4)]
    partners = [at(y_=y_off(o)) for o in (1, 3, 2)]
    partners += [sibling]
    partners += [at(z_=other) for other in near_z + flip_z]
    partners += [at(x_=x_pair, z_=other) for other in z_all]
    partners += [at(x_=far, z_=other) for far in x_far for other in [z] + near_z]

    barrier = pltpu.get_barrier_semaphore()
    for other in partners:
        pl.semaphore_signal(barrier, inc=1, device_id=other, device_id_type=MESH)

    copies = []

    def send(src, dst, target):
        i = len(copies)
        copy = pltpu.make_async_remote_copy(
            src_ref=src, dst_ref=dst, send_sem=send_sem.at[i], recv_sem=recv_sem.at[i],
            device_id=target, device_id_type=MESH,
        )
        copies.append(copy)
        copy.start()
        return copy

    def recv(copy):
        copy.wait_recv()

    def fetch(i, src, dst):
        copy = pltpu.make_async_copy(src, dst, local_sem.at[i])
        copy.start()
        return copy

    got_order = fetch(1, order_ref, order)
    got_loads = fetch(0, loads_ref, blocks.at[3])
    got_left = fetch(2, left_ref, left)
    got_right = fetch(3, right_ref, right)

    pl.semaphore_wait(barrier, len(partners))

    def columns(ref, start, count):
        return ref.at[:, pl.ds(start, count)]

    up, down = at(y_=y_off(1)), at(y_=y_off(3))
    up_first = send(columns(loads_ref, 0, HALF), columns(blocks.at[0], 0, HALF), up)
    down_first = send(columns(loads_ref, HALF, HALF), columns(blocks.at[1], HALF, HALF), down)
    up_second = send(columns(loads_ref, HALF, HALF), columns(blocks.at[0], HALF, HALF), up)
    down_second = send(columns(loads_ref, 0, HALF), columns(blocks.at[1], 0, HALF), down)
    size = size_ref[0]
    first_row = fac * ROWS
    got_left.wait()
    got_right.wait()
    for level in range(LEVELS):
        live = first_row + lax.broadcasted_iota(jnp.int32, (RANK, ROWS), 1) < size
        turned = left[level].T
        left_t[core, level * RANK:(level + 1) * RANK, :] = jnp.where(live, turned, jnp.zeros_like(turned))
        right_w[core, :, level * RANK:(level + 1) * RANK] = right[level]
    mix[:, :2 * RANK] = jnp.dot(left_t[core, :RANK, :], right_w[core, :, RANK:], preferred_element_type=jnp.float32)
    mix[:, 2 * RANK:] = jnp.dot(
        left_t[core, RANK:2 * RANK, :], right_w[core, :, 2 * RANK:], preferred_element_type=jnp.float32
    )
    mix_sib = send(mix.at[rows_of(64 * (1 - core), 64), :], mix_core, sibling)

    inverse_sib = send(inverse_ref, inverse.at[core], sibling)
    right_sib = send(right_w.at[core], right_w.at[core], sibling)
    left_sib = send(left_t.at[core], left_t.at[core], sibling)
    got_inverse = fetch(4, inverse_ref, inverse.at[core])

    got_order.wait()

    place = lax.broadcasted_iota(jnp.int32, (32, 128), 0) * 128 + lax.broadcasted_iota(jnp.int32, (32, 128), 1)
    turned = jnp.where(place < size, order[...], -1).T
    for r in range(32):
        match[r * 128:(r + 1) * 128, :] = jnp.broadcast_to(turned[:, r:r + 1], (128, 128))

    owners = [y_off(3) * 2 + core, y_off(1) * 2 + core, y_off(2) * 2 + core, fac]

    def permute(parts, first=False, tall=2048):
        @pl.loop(0, SLOTS // tall)
        def _(m):
            rows = pl.ds(pl.multiple_of(m * tall, tall), tall)
            slot = match[rows, :]
            picks, held = [], []
            for block, start, count in parts:
                held.append(blocks[block, :, start:start + count])
                for j in range(count // 128):
                    here = owners[block] * ROWS + start + j * 128
                    column = here + lax.broadcasted_iota(jnp.int32, (tall, 128), 1)
                    picks.append(jnp.where(slot == column, 1.0, 0.0).astype(jnp.bfloat16))
            held = held[0] if len(held) == 1 else jnp.concatenate(held, axis=1)
            total = lax.dot_general(
                jnp.concatenate(picks, axis=1), held, (((1,), (1,)), ((), ())),
                preferred_element_type=jnp.float32,
            )
            total = total.astype(jnp.bfloat16)
            if first:
                ordered[rows, :] = total
            else:
                ordered[rows, :] += total

    recv(mix_sib)
    mix_half[...] = mix[rows_of(64 * core, 64), :] + mix_core[...]
    to_z = []
    for o in range(4):
        rows = rows_of(16 * lax.rem(z_lo + o, 4), 16)
        to_z.append(send(mix_half.at[rows, pl.ds(0, 2 * RANK)], mix_near.at[o], at(z_=z_off(o, 1))))
        for f in range(2):
            to_z.append(send(
                mix_half.at[rows, pl.ds(2 * RANK, RANK)], mix_far.at[f * 4 + o],
                at(x_=x_pair, z_=z_off(o, f)),
            ))

    got_loads.wait()
    permute([(3, 0, ROWS)], first=True)

    forwards = []
    quarter = HALF // 2
    recv(up_first)
    for j in range(2):
        here = j * quarter
        forwards.append(send(columns(blocks.at[0], here, quarter), columns(blocks.at[2], here, quarter), up))
    recv(down_first)
    for j in range(2):
        here = HALF + (1 - j) * quarter
        forwards.append(send(columns(blocks.at[1], here, quarter), columns(blocks.at[2], here, quarter), down))
    permute([(0, 0, HALF), (1, HALF, HALF)])

    recv(up_second)
    recv(down_second)
    permute([(0, HALF, HALF), (1, 0, HALF)])

    for copy in to_z:
        recv(copy)
    mix_z[:, :2 * RANK] = mix_near[0] + mix_near[1] + mix_near[2] + mix_near[3]
    far = mix_far[0]
    for j in range(1, 8):
        far = far + mix_far[j]
    mix_z[:, 2 * RANK:] = far
    mix_across = [send(mix_z, mix_y.at[o], at(y_=y_off(o))) for o in (1, 2, 3)]

    recv(forwards[0])
    recv(forwards[2])
    recv(forwards[1])
    recv(forwards[3])
    permute([(2, 0, ROWS)])

    got_inverse.wait()
    recv(inverse_sib)
    base = len(copies)

    def swap(b):
        return pltpu.make_async_remote_copy(
            src_ref=partial.at[1 - core, b], dst_ref=from_core.at[b], send_sem=send_sem.at[base + b],
            recv_sem=recv_sem.at[base + b], device_id=sibling, device_id_type=MESH,
        )

    @pl.loop(0, 2)
    def _(b):
        solved = jnp.dot(inverse[b], ordered[...], preferred_element_type=jnp.float32)
        for h in range(2):
            partial[h, b] = solved[:, 128 * h:128 * h + 128]
        swap(b).start()

    to_core = [swap(0), swap(1)]
    copies += to_core
    for copy in mix_across:
        recv(copy)
    mine = rows_of(64 * core + 16 * z_lo, 16)
    mixing[mine, :] = mix_z[...] + mix_y[1] + mix_y[2] + mix_y[3]
    spread = [send(mixing.at[mine, :], mixing.at[mine, :], at(z_=other)) for other in near_z]

    def settle(b):
        live = y * 2 * ROWS + b * ROWS + lax.broadcasted_iota(jnp.int32, (ROWS, 128), 0) < size
        field[b] = jnp.where(live, partial[core, b] + from_core[b], 0.0).T

    def halves(value):
        high = value.astype(jnp.bfloat16)
        return high, (value - high.astype(jnp.float32)).astype(jnp.bfloat16)

    def split_dot(value, weight):
        high, low = halves(value)
        return jnp.dot(high, weight, preferred_element_type=jnp.float32) + jnp.dot(
            low, weight, preferred_element_type=jnp.float32
        )

    recv(right_sib)
    coef_core[...] = jnp.zeros((128, WIDE), jnp.float32)

    @pl.loop(0, 2)
    def _(b):
        swap(b).wait_recv()
        settle(b)
        coef_core[...] += split_dot(field[b], right_w[b])

    pair = lax.div(z_lo, 2)
    to_y = []
    for part in (1 - pair, pair):
        for o in (2, 1, 3):
            rows = rows_of(32 * y_off(o) + 16 * part, 16)
            to_y.append(send(coef_core.at[rows, :], in_y.at[o, rows_of(16 * part, 16), :], at(y_=y_off(o))))
    for copy in spread:
        recv(copy)
    sixty_four = mixing.at[rows_of(64 * core, 64), :]
    spread = send(sixty_four, sixty_four, sibling)

    def z_flip(o):
        return [z_lo, z_lo + 1 - 2 * lax.rem(z_lo, 2), lax.rem(z_lo + 2, 4), 3 - z_lo][o]

    def mixed(value, start, count):
        high, low = halves(value)
        both = jnp.concatenate([high, low], axis=0)
        by_high = jnp.dot(both, mix_split[:, start:start + count], preferred_element_type=jnp.float32)
        by_low = jnp.dot(both, mix_split[:, WIDE + start:WIDE + start + count], preferred_element_type=jnp.float32)
        return by_high[:16] + (by_high[16:] + by_low[:16])

    recv(spread)
    mix_split[:, :WIDE], mix_split[:, WIDE:] = halves(mixing[...])
    to_node = []
    for n, part in enumerate((1 - pair, pair)):
        for copy in to_y[3 * n:3 * n + 3]:
            recv(copy)
        rows = rows_of(16 * part, 16)
        summed = coef_core[rows_of(32 * y + 16 * part, 16), :] + in_y[1, rows, :] + in_y[2, rows, :] + in_y[3, rows, :]
        zero = summed[:, :RANK]
        terms = mixed(zero, 0, 2 * RANK)
        one = summed[:, RANK:2 * RANK] + terms[:, :RANK]
        two = summed[:, 2 * RANK:] + terms[:, RANK:] + mixed(one, 2 * RANK, RANK)
        coef_y[rows, :] = jnp.concatenate([zero, one, two], axis=1)
        for o in ((2, 3), (0, 1))[n]:
            eight = rows_of(8 * z_flip(o), 8)
            there = z_hi * 4 + z_flip(o)
            for g, far in enumerate(x_far):
                to_node.append(send(coef_y.at[eight, pl.ds(2 * RANK, RANK)], in_two.at[o, g], at(x_=far, z_=there)))
            to_node.append(send(coef_y.at[eight, pl.ds(RANK, RANK)], in_one.at[o], at(x_=x_pair, z_=there)))
            if o:
                to_node.append(send(coef_y.at[eight, pl.ds(0, RANK)], in_zero.at[o], at(z_=there)))
    for copy in to_node:
        recv(copy)
    node[:, :RANK] = coef_y[rows_of(8 * z_lo, 8), :RANK] + (in_zero[1] + in_zero[2] + in_zero[3])
    node[:, RANK:2 * RANK] = (in_one[0] + in_one[1]) + (in_one[2] + in_one[3])
    node[:, 2 * RANK:] = ((in_two[0, 0] + in_two[1, 0]) + (in_two[2, 0] + in_two[3, 0])) + (
        (in_two[0, 1] + in_two[1, 1]) + (in_two[2, 1] + in_two[3, 1])
    )
    over = [send(node, in_flip.at[o], at(z_=z_off(o, 1))) for o in range(4)]
    wide = pl.ds(RANK, 2 * RANK)
    over += [send(node.at[:, wide], in_near.at[o], at(z_=z_off(o))) for o in (1, 2, 3)]
    for copy in over:
        recv(copy)
    for o in range(4):
        eight = rows_of(32 * y + 8 * lax.rem(z_lo + 4 - o, 4), 8)
        beside = node[:, RANK:] if o == 0 else in_near[o]
        partner[eight, :RANK] = in_flip[o, :, :RANK]
        partner[eight, RANK:] = in_flip[o, :, RANK:] + beside

    thirty_two = partner.at[rows_of(32 * y, 32), :]
    back = [send(thirty_two, thirty_two, at(y_=y_off(o))) for o in (2, 1, 3)]
    recv(left_sib)
    for copy in back:
        recv(copy)
    ours = rows_of(128 * core, 128)
    out_far[...] = field[1 - core] + split_dot(partner[...], left_t[1 - core])
    to_out = send(out_far, out_ref.at[ours, :], sibling)
    out_ref[ours, :] = field[core] + split_dot(partner[...], left_t[core])
    recv(to_out)
    for copy in copies:
        copy.wait_send()


def body(loads, leaf_sizes, tree_order, leaf_inverse, left_factors, right_factors):
    f32, bf16 = jnp.float32, jnp.bfloat16
    scratch = [
        ((4, CASES, ROWS), bf16),
        ((32, 128), jnp.int32),
        ((SLOTS, 128), jnp.int32),
        ((SLOTS, CASES), bf16),
        ((2, ROWS, SLOTS), bf16),
        ((LEVELS, ROWS, RANK), bf16),
        ((LEVELS, ROWS, RANK), bf16),
        ((2, WIDE, ROWS), bf16),
        ((2, ROWS, WIDE), bf16),
        ((2, 2, ROWS, 128), f32),
        ((2, ROWS, 128), f32),
        ((2, 128, ROWS), f32),
        ((128, WIDE), f32),
        ((4, 32, WIDE), f32),
        ((32, WIDE), f32),
        ((8, WIDE), f32),
        ((4, 8, WIDE), f32),
        ((4, 8, 2 * RANK), f32),
        ((4, 8, RANK), f32),
        ((4, 8, RANK), f32),
        ((4, 2, 8, RANK), f32),
        ((128, WIDE), f32),
        ((128, ROWS), f32),
        ((RANK, WIDE), f32),
        ((64, WIDE), f32),
        ((64, WIDE), f32),
        ((4, 16, 2 * RANK), f32),
        ((8, 16, RANK), f32),
        ((16, WIDE), f32),
        ((4, 16, WIDE), f32),
        ((RANK, WIDE), f32),
        ((RANK, 2 * WIDE), bf16),
    ]
    in_hbm = pl.BlockSpec(memory_space=pltpu.HBM)
    return pl.pallas_call(
        kernel,
        out_shape=pltpu.VMEM((CASES, ROWS), f32),
        in_specs=[
            in_hbm, pl.BlockSpec(memory_space=pltpu.SMEM), in_hbm, in_hbm, in_hbm, in_hbm,
        ],
        out_specs=pl.BlockSpec(memory_space=pltpu.VMEM),
        scratch_shapes=[pltpu.VMEM(shape, dtype) for shape, dtype in scratch] + [
            pltpu.SemaphoreType.DMA((5,)),
            pltpu.SemaphoreType.DMA((COPIES,)),
            pltpu.SemaphoreType.DMA((COPIES,)),
        ],
        compiler_params=pltpu.CompilerParams(
            collective_id=0, has_side_effects=True, vmem_limit_bytes=60 << 20
        ),
    )(loads, leaf_sizes, tree_order.reshape(32, 128), leaf_inverse, left_factors, right_factors)


def solution(mesh):
    placed = (
        P(None, ("leaf", "fac")),
        P("leaf"),
        P("leaf", None),
        P(("leaf", "fac"), None),
        P(None, ("leaf", "fac"), None),
        P(None, ("leaf", "fac"), None),
    )
    return jax.shard_map(
        body, mesh=mesh, in_specs=placed, out_specs=P(None, ("leaf", "fac")), check_vma=False
    )
```
